32 devices in a mesh: freq: 4 (over y, x), tm: 8 (over z, core).
Axes of the slice: x: 2, y: 2, z: 4, core: 2. Of those that a mesh axis runs over, the one named last changes fastest.
Arguments:
- visibilities: bfloat16 [4, 8, 2, 512, 512], P('freq', 'tm'), may hold values from -1.796875 to 1.796875
- model_vis: bfloat16 [4, 8, 2, 512, 512], P('freq'), may hold values from -0.1796875 to 0.1796875
- station_flags: int32 [4, 8, 512], P('freq', 'tm'), may hold values 0 or 1
- initial_gains: float32 [4, 8, 2, 8, 512], P('freq', 'tm'), may hold values from -6 to 6
- initial_duals: float32 [4, 8, 2, 8, 512], P('freq', 'tm'), may hold values from -1.8 to 1.8
Outputs:
- solved_gains: float32 [4, 8, 2, 8, 512], P('freq', 'tm')
- consensus: float32 [4, 8, 2, 8, 512], P('freq', 'tm')
- final_duals: float32 [4, 8, 2, 8, 512], P('freq', 'tm')
The draws below stay inside these ranges and needn't reach their ends.
All inputs are finite; a program needn't handle non-finite values. No bound on the sum of `station_flags` on one device may be relied on, other than what follows from the above.
Results may differ from the reference program's by a relative error of at most 0.0003.
Values sent between devices are 32-bit elements; how exact they have to be, the bound alone decides.
No kernel may reach another device: no remote copies, remote signals or barrier semaphores. Data moves between devices by JAX's collectives and lax.ppermute only.
A program may use at most 64 MiB of HBM per device.

```python
import math
import jax
import jax.numpy as jnp
from jax import lax

DIRS = 8
ITERS = 2
NR = 512
NF = 4
NT = 8
N_FREQ = 4
N_TM = 8


def touch_ends(array, rng, smallest, largest):
    place = [jax.random.randint(jax.random.fold_in(rng, axis), (), 0, length) for axis, length in enumerate(array.shape)]
    widest = array.shape.index(max(array.shape))
    next_to = place[:widest] + [(place[widest] + 1) % array.shape[widest]] + place[widest + 1:]
    return array.at[tuple(place)].set(smallest).at[tuple(next_to)].set(largest)


def level_of(key, extent, shards, least, high):
    def one(axis_at, blocks):
        draws = jax.random.uniform(jax.random.fold_in(jax.random.fold_in(key, 6), axis_at), (blocks,), jnp.float32, least / len(shards), high / len(shards))
        return jnp.repeat(jnp.exp(draws), extent[axis_at] // blocks).reshape((-1,) + (1,) * (len(extent) - axis_at - 1))

    loudness = one(*shards[0])
    for cut in shards[1:]:
        loudness = loudness * one(*cut)
    return loudness


def normal_values(stream_key, dims, scale, limit, pieces=(), held_as=jnp.bfloat16):
    result = jax.random.normal(stream_key, dims, jnp.float32) * scale
    if len(pieces) > 0:
        result = level_of(stream_key, dims, pieces, -0.22, 0.18) * result
    return jnp.clip(result, min=-limit, max=limit).astype(held_as)


def setup_inputs(seed: int = 0) -> dict:
    splits = jax.random.split(jax.random.key(seed), 6)
    visibilities = normal_values(splits[0], (NF, NT, 2, NR, NR), 0.3, 1.796875, ((0, 4), (1, 8)))
    model_vis = normal_values(splits[1], (NF, DIRS, 2, NR, NR), 0.03, 0.1796875, ((0, 4),))
    station_flags = touch_ends((jax.random.randint(splits[2], (NF, NT, NR), 0, 16) < 15).astype(jnp.int32), jax.random.fold_in(splits[2], 1), 0, 1)
    initial_gains = normal_values(splits[3], (NF, NT, 2, DIRS, NR), 1.0, 6.0, ((0, 4), (1, 8)), jnp.float32)
    initial_duals = normal_values(splits[4], (NF, NT, 2, DIRS, NR), 0.3, 1.8, ((0, 4), (1, 8)), jnp.float32)
    return {"visibilities": visibilities, "model_vis": model_vis, "station_flags": station_flags, "initial_gains": initial_gains, "initial_duals": initial_duals}


penalty = 1.0

def poly_basis(length, position, order_count):
    centre = position - (length - 1) / 2.0
    constant = jnp.ones_like(position) / math.sqrt(length)
    linear = centre / math.sqrt(length * (length * length - 1) / 12.0)
    stacked = [constant, linear]
    if order_count == 3:
        quadratic = (centre * centre - (length * length - 1) / 12.0) / math.sqrt(length * (length * length - 1) * (length * length - 4) / 180.0)
        stacked.append(quadratic)
    return jnp.stack(stacked, axis=0)

def local_solve(vis_block, model_block, flag_block, gains_block, target_block):
    real_vis = vis_block[0].astype(jnp.float32)
    imag_vis = vis_block[1].astype(jnp.float32)
    model_real = model_block[:, 0].astype(jnp.float32)
    model_imag = model_block[:, 1].astype(jnp.float32)
    gain_real = gains_block[0]
    gain_imag = gains_block[1]
    weight = flag_block.astype(jnp.float32)
    outer_real = gain_real[:, :, None] * gain_real[:, None, :] + gain_imag[:, :, None] * gain_imag[:, None, :]
    outer_imag = gain_imag[:, :, None] * gain_real[:, None, :] - gain_real[:, :, None] * gain_imag[:, None, :]
    pred_real = lax.optimization_barrier(jnp.sum(model_real * outer_real - model_imag * outer_imag, axis=0))
    pred_imag = lax.optimization_barrier(jnp.sum(model_real * outer_imag + model_imag * outer_real, axis=0))
    pair_weight = weight[:, None] * weight[None, :]
    resid_real = (real_vis - pred_real) * pair_weight
    resid_imag = (imag_vis - pred_imag) * pair_weight
    proj_real = model_real * gain_real[:, None, :] + model_imag * gain_imag[:, None, :]
    proj_imag = model_real * gain_imag[:, None, :] - model_imag * gain_real[:, None, :]
    numer_real = lax.optimization_barrier(jnp.sum(resid_real[None] * proj_real - resid_imag[None] * proj_imag, axis=2))
    numer_imag = lax.optimization_barrier(jnp.sum(resid_real[None] * proj_imag + resid_imag[None] * proj_real, axis=2))
    gain_power = (gain_real * gain_real + gain_imag * gain_imag) * weight
    curvature = weight[None, :] * lax.optimization_barrier(jnp.sum((model_real * model_real + model_imag * model_imag) * gain_power[:, None, :], axis=2))
    divisor = curvature + penalty
    new_real = (numer_real + curvature * gain_real + penalty * target_block[0]) / divisor
    new_imag = (numer_imag + curvature * gain_imag + penalty * target_block[1]) / divisor
    return jnp.stack([new_real, new_imag], axis=0)

def solve_all(visibilities, model_vis, station_flags, current, target):

    def one_block(block_index):
        freq_place = block_index // N_TM
        time_place = block_index % N_TM
        return local_solve(visibilities[freq_place, time_place], model_vis[freq_place], station_flags[freq_place, time_place], current[freq_place, time_place], target[freq_place, time_place])
    solved = lax.map(one_block, jnp.arange(N_FREQ * N_TM, dtype=jnp.int32))
    return solved.reshape(current.shape)

def reference(visibilities, model_vis, station_flags, initial_gains, initial_duals):
    freq_basis = poly_basis(N_FREQ, jnp.arange(N_FREQ).astype(jnp.float32), 3)
    time_basis = poly_basis(N_TM, jnp.arange(N_TM).astype(jnp.float32), 2)
    current = initial_gains
    scaled_dual = initial_duals
    consensus = initial_gains
    for iteration in range(ITERS):
        merged = (current + scaled_dual).reshape(N_FREQ, N_TM, -1)
        coeffs = jnp.einsum('if,jt,ftx->ijx', freq_basis, time_basis, merged, precision=lax.Precision.HIGHEST)
        consensus = jnp.einsum('if,jt,ijx->ftx', freq_basis, time_basis, coeffs, precision=lax.Precision.HIGHEST).reshape(current.shape)
        scaled_dual = scaled_dual + current - consensus
        target = consensus - scaled_dual
        current = solve_all(visibilities, model_vis, station_flags, current, target)
    return (current, consensus, scaled_dual)
```

```python
import functools
import math

import jax
import jax.numpy as jnp
from jax import lax
from jax.experimental import pallas as pl
from jax.experimental.pallas import tpu as pltpu
from jax.sharding import PartitionSpec as P

ITERS = 2
LANES = 128
ROWS = 16
FREQ_ORDERS = 3
TIME_ORDERS = 2

penalty = 1.0
f32 = jnp.float32


def poly_basis(length, position, order_count):
    centre = position - (length - 1) / 2.0
    stacked = [jnp.ones_like(position) * (1.0 / math.sqrt(length)), centre * (1.0 / math.sqrt(length * (length * length - 1) / 12.0))]
    if order_count == 3:
        scale = math.sqrt(length * (length * length - 1) * (length * length - 4) / 180.0)
        stacked.append((centre * centre - (length * length - 1) / 12.0) * (1.0 / scale))
    return stacked


def whole_vmem(count):
    return [pl.BlockSpec(memory_space=pltpu.VMEM)] * count


def exchange(array, axis, distance):
    size = lax.axis_size(axis)
    return lax.ppermute(array, axis, [(place, place ^ distance) for place in range(size)])


def axis_plan(size, orders, distances):
    steps = []
    held, sums = 1, False
    for at in range(len(distances)):
        if at == len(distances) - 1:
            steps.append((1, False, held, sums))
            break
        sent = held
        if sums:
            steps.append((sent, False, held, sums))
            continue
        held = 2 * held
        turn = held > orders and at < len(distances) - 2
        steps.append((sent, turn, held, sums))
        if turn:
            held, sums = orders, True
    return steps


def heard_places(index, distances):
    places = [index]
    for distance in distances:
        places = places + [place ^ distance for place in places]
    return places


def axis_weights(size, orders, distances, index):
    weights = []

    def basis(place):
        return poly_basis(size, lax.convert_element_type(place, f32), orders)

    def products(one, other):
        return sum(a * b for a, b in zip(one, other))

    plan = axis_plan(size, orders, distances)
    raw = [index]
    for at, (sent, turn, held, sums) in enumerate(plan):
        if at == len(plan) - 1:
            for target in (index ^ distances[at], index):
                if sums:
                    weights += basis(target)
                else:
                    weights += [products(basis(target), basis(place)) for place in raw]
        elif not sums:
            raw = raw + [place ^ distances[at] for place in raw]
            if turn:
                for place in raw:
                    weights += basis(place)
    return weights


def weight_count(size, orders, distances):
    total, raw = 0, 1
    plan = axis_plan(size, orders, distances)
    for at, (sent, turn, held, sums) in enumerate(plan):
        if at == len(plan) - 1:
            total += 2 * (orders if sums else raw)
        elif not sums:
            raw *= 2
            if turn:
                total += raw * orders
    return total


def tied(array, others):
    return lax.optimization_barrier((array, others))


class Work:
    def __init__(self, parts):
        self.parts = parts
        self.results = []

    def beside(self, sent):
        part = self.parts[len(self.results)]
        result, sent = part(sent)
        self.results.append(result)
        return result


def axis_exchange(state, axis, orders, distances, weights, work, finish):
    size = lax.axis_size(axis)
    plan = axis_plan(size, orders, distances)
    weights = list(weights)
    held = [state]
    for at, (sent, turn, _, sums) in enumerate(plan):
        if at == len(plan) - 1:
            away = weights[: len(held)]
            own = weights[len(held) :]
            message = sum(w * a for w, a in zip(away, held))
            got = work(message, axis, distances[at])
            if not finish:
                return None, list(zip(own, held)), got
            return sum(w * a for w, a in zip(own, held)) + got, None, None
        message = held[0] if len(held) == 1 else jnp.stack(held)
        got = work(message, axis, distances[at])
        got = [got] if len(held) == 1 else [got[i] for i in range(len(held))]
        if sums:
            held = [a + b for a, b in zip(held, got)]
            continue
        held = held + got
        if turn:
            taken, weights = weights[: len(held) * orders], weights[len(held) * orders :]
            held = [sum(taken[i * orders + j] * a for i, a in enumerate(held)) for j in range(orders)]


def setup_kernel(plans, gains_ref, duals_ref, flags_ref, merged_ref, masked_ref, turned_ref, mask_ref, *weight_refs):
    gains = gains_ref[...]
    mask = flags_ref[...].astype(f32)
    mask_ref[...] = mask
    merged_ref[...] = gains + duals_ref[...]
    masked_ref[...] = gains * mask[None]
    turned_ref[...] = turn(gains)
    at = 0
    shape = weight_refs[0].shape
    for axis, size, orders, distances in plans:
        index = jnp.full((8, LANES), lax.axis_index(axis), jnp.int32)
        for weight in axis_weights(size, orders, distances, index):
            weight_refs[at][...] = jnp.broadcast_to(jnp.tile(weight, (shape[1] // 8, shape[2] // LANES))[None], shape)
            at += 1


def turn(gains):
    flat = gains.reshape(-1, gains.shape[-1])
    padded = jnp.concatenate([flat, jnp.zeros((LANES - flat.shape[0], flat.shape[1]), f32)], axis=0)
    return padded.T


def part_kernel(start, unroll, model_ref, vis_ref, masked_ref, turned_ref, sums_ref):
    directions = model_ref.shape[0]
    receptors = model_ref.shape[3]

    def rows_of(at, carry):
        first = pl.multiple_of(at * ROWS, ROWS)
        rows = pl.ds(pl.multiple_of(start + first, ROWS), ROWS)
        turned = turned_ref[rows, :]
        near = [jnp.broadcast_to(turned[:, k : k + 1], (ROWS, LANES)) for k in range(2 * directions)]
        sums = [None] * (3 * directions)
        for block in range(receptors // LANES):
            columns = pl.ds(block * LANES, LANES)
            resid_real = vis_ref[0, rows, columns].astype(f32)
            resid_imag = vis_ref[1, rows, columns].astype(f32)
            moved = []
            for k in range(directions):
                model_real = model_ref[k, 0, rows, columns].astype(f32)
                model_imag = model_ref[k, 1, rows, columns].astype(f32)
                gain_real = masked_ref[0, k : k + 1, columns]
                gain_imag = masked_ref[1, k : k + 1, columns]
                moved_real = model_real * gain_real + model_imag * gain_imag
                moved_imag = model_imag * gain_real - model_real * gain_imag
                moved.append((moved_real, moved_imag))
                resid_real = resid_real - (near[k] * moved_real - near[directions + k] * moved_imag)
                resid_imag = resid_imag - (near[k] * moved_imag + near[directions + k] * moved_real)
            for k, (moved_real, moved_imag) in enumerate(moved):
                terms = (
                    resid_real * moved_real + resid_imag * moved_imag,
                    resid_imag * moved_real - resid_real * moved_imag,
                    moved_real * moved_real + moved_imag * moved_imag,
                )
                for kind, term in enumerate(terms):
                    place = kind * directions + k
                    sums[place] = term if block == 0 else sums[place] + term
        lane = lax.broadcasted_iota(jnp.int32, (ROWS, LANES), 1)
        out = jnp.zeros((ROWS, LANES), f32)
        for place, total in enumerate(sums):
            out = jnp.where(lane == place, jnp.sum(total, axis=1, keepdims=True), out)
        sums_ref[pl.ds(first, ROWS), :] = out
        return carry

    lax.fori_loop(0, sums_ref.shape[0] // ROWS, rows_of, 0, unroll=unroll)


def update_kernel(parts, terms, last, *refs):
    sums_refs, refs = refs[:parts], refs[parts:]
    weight_refs, held_refs, refs = refs[:terms], refs[terms : 2 * terms], refs[2 * terms :]
    got_ref, merged_ref, gains_ref, mask_ref = refs[:4]
    outs = refs[4:]
    sums = jnp.concatenate([ref[...] for ref in sums_refs], axis=0).T
    gains = gains_ref[...]
    mask = mask_ref[...]
    directions = gains.shape[1]
    consensus = got_ref[...]
    for weight_ref, held_ref in zip(weight_refs, held_refs):
        consensus = consensus + weight_ref[...] * held_ref[...]
    duals = merged_ref[...] - consensus
    target = consensus - duals
    curvature = sums[2 * directions : 3 * directions] * mask
    divisor = curvature + penalty
    solved = []
    for part in range(2):
        numer = sums[part * directions : (part + 1) * directions] * mask
        solved.append((numer + curvature * gains[part] + penalty * target[part]) / divisor)
    solved = jnp.stack(solved)
    if last:
        for ref, value in zip(outs, (solved, consensus, duals)):
            ref[...] = value
    else:
        for ref, value in zip(outs, (solved, solved + duals, solved * mask[None], turn(solved))):
            ref[...] = value


def cut(total, shares):
    whole = sum(shares)
    ends = [0]
    done = 0.0
    for share in shares:
        done += share
        ends.append(round(total * done / whole))
    return [max(0, b - a) for a, b in zip(ends, ends[1:])]


def per_device(visibilities, model_vis, station_flags, initial_gains, initial_duals):
    vis_block = visibilities[0, 0]
    model_block = model_vis[0]
    flag_block = station_flags[0]
    gains = initial_gains[0, 0]
    duals = initial_duals[0, 0]
    _, directions, receptors = gains.shape
    state = jax.ShapeDtypeStruct(gains.shape, f32)
    turned_shape = jax.ShapeDtypeStruct((receptors, LANES), f32)

    freq_count, time_count = lax.axis_size("freq"), lax.axis_size("tm")
    freq_steps = [1 << b for b in range(freq_count.bit_length() - 1)]
    time_steps = [1 << b for b in reversed(range(time_count.bit_length() - 1))]
    plans = (
        ("freq", freq_count, FREQ_ORDERS, tuple(freq_steps)),
        ("tm", time_count, TIME_ORDERS, tuple(time_steps)),
    )
    counts = [weight_count(*plan[1:]) for plan in plans]

    merged, masked, turned, mask, *weights = pl.pallas_call(
        functools.partial(setup_kernel, plans),
        out_shape=[state, state, turned_shape, jax.ShapeDtypeStruct((1, receptors), f32)] + [state] * sum(counts),
        in_specs=whole_vmem(3),
        out_specs=whole_vmem(4 + sum(counts)),
        compiler_params=pltpu.CompilerParams(vmem_limit_bytes=16 * 2**20),
        name="setup",
    )(gains, duals, flag_block)
    freq_weights, time_weights = weights[: counts[0]], weights[counts[0] :]

    steps = len(freq_steps) + len(time_steps)
    shares = [1.0] * (steps - 1) + [0.45]
    lengths = [ROWS * units for units in cut(receptors // ROWS, shares)]
    starts = [sum(lengths[:i]) for i in range(steps)]
    pairs = directions * receptors

    def part(number, masked, turned):
        length = lengths[number]
        return pl.pallas_call(
            functools.partial(part_kernel, starts[number], 4),
            out_shape=jax.ShapeDtypeStruct((length, LANES), f32),
            in_specs=whole_vmem(4),
            out_specs=pl.BlockSpec(memory_space=pltpu.VMEM),
            compiler_params=pltpu.CompilerParams(vmem_limit_bytes=32 * 2**20),
            cost_estimate=pl.CostEstimate(flops=28 * pairs * length, bytes_accessed=4 * pairs * length, transcendentals=0),
            name=f"part{number}",
        )(model_block, vis_block, masked, turned)

    for iteration in range(ITERS):
        last = iteration == ITERS - 1
        results = []

        def work(message, axis, distance):
            message, one, two = lax.optimization_barrier((message, masked, turned))
            got = exchange(message, axis, distance)
            result = part(len(results), one, two)
            got, result = lax.optimization_barrier((got, result))
            results.append(result)
            return got

        along_freq, _, _ = axis_exchange(merged, "freq", FREQ_ORDERS, freq_steps, freq_weights, work, True)
        _, terms, got = axis_exchange(along_freq, "tm", TIME_ORDERS, time_steps, time_weights, work, False)
        outs = [state] * 3 + ([] if last else [turned_shape])
        operands = results + [w for w, _ in terms] + [a for _, a in terms] + [got, merged, gains, mask]
        outputs = pl.pallas_call(
            functools.partial(update_kernel, len(results), len(terms), last),
            out_shape=outs,
            in_specs=whole_vmem(len(operands)),
            out_specs=whole_vmem(len(outs)),
            compiler_params=pltpu.CompilerParams(vmem_limit_bytes=16 * 2**20),
            name="finish" if last else "update",
        )(*operands)
        if last:
            return tuple(out[None, None] for out in outputs)
        gains, merged, masked, turned = outputs


def solution(mesh):
    in_specs = (
        P("freq", "tm", None, None, None),
        P("freq", None, None, None, None),
        P("freq", "tm", None),
        P("freq", "tm", None, None, None),
        P("freq", "tm", None, None, None),
    )
    out_specs = (
        P("freq", "tm", None, None, None),
        P("freq", "tm", None, None, None),
        P("freq", "tm", None, None, None),
    )
    return jax.shard_map(
        per_device, mesh=mesh, in_specs=in_specs, out_specs=out_specs, check_vma=False
    )
```

```python
import functools
import math

import jax
import jax.numpy as jnp
from jax import lax
from jax.experimental import pallas as pl
from jax.experimental.pallas import tpu as pltpu
from jax.sharding import PartitionSpec as P

LANES = 128
ROWS = 16
FREQ_ORDERS = 3
TIME_ORDERS = 2
MIB = 2**20

penalty = 1.0
f32 = jnp.float32


def poly_basis(length, position, order_count):
    centre = position - (length - 1) / 2.0
    linear = centre * (1.0 / math.sqrt(length * (length * length - 1) / 12.0))
    stacked = [jnp.ones_like(position) * (1.0 / math.sqrt(length)), linear]
    if order_count == 3:
        scale = math.sqrt(length * (length * length - 1) * (length * length - 4) / 180.0)
        stacked.append((centre * centre - (length * length - 1) / 12.0) * (1.0 / scale))
    return stacked


def whole_vmem(count):
    return [pl.BlockSpec(memory_space=pltpu.VMEM)] * count


def exchange(array, axis, distance):
    size = lax.axis_size(axis)
    return lax.ppermute(array, axis, [(place, place ^ distance) for place in range(size)])


def time_plan(distances):
    steps = []
    held, sums = 1, False
    for at in range(len(distances)):
        last = at == len(distances) - 1
        turn = not last and not sums and 2 * held > TIME_ORDERS and at < len(distances) - 2
        steps.append((held, sums, turn))
        if turn:
            held, sums = TIME_ORDERS, True
        elif not sums:
            held = 2 * held
    return steps


def time_weights(size, distances, index):
    weights = []

    def basis(place):
        return poly_basis(size, lax.convert_element_type(place, f32), TIME_ORDERS)

    def product(one, other):
        return sum(a * b for a, b in zip(basis(one), basis(other)))

    raw = [index]
    for at, (held, sums, turn) in enumerate(time_plan(distances)):
        if at == len(distances) - 1:
            for target in (index ^ distances[at], index):
                weights += basis(target) if sums else [product(target, place) for place in raw]
        elif not sums:
            raw = raw + [place ^ distances[at] for place in raw]
            if turn:
                for place in raw:
                    weights += basis(place)
    return weights


def time_weight_count(distances):
    total, raw = 0, 1
    for at, (held, sums, turn) in enumerate(time_plan(distances)):
        if at == len(distances) - 1:
            total += 2 * held
        elif not sums:
            raw = 2 * raw
            total += raw * TIME_ORDERS if turn else 0
    return total


def time_exchange(state, distances, weights, work):
    weights = list(weights)
    held = [state]
    for at, (_, sums, turn) in enumerate(time_plan(distances)):
        if at == len(distances) - 1:
            away, own = weights[: len(held)], weights[len(held) :]
            got = work(at, sum(w * a for w, a in zip(away, held)), distances[at])
            return held, own, got
        message = held[0] if len(held) == 1 else jnp.stack(held)
        got = work(at, message, distances[at])
        got = [got] if len(held) == 1 else [got[i] for i in range(len(held))]
        if sums:
            held = [a + b for a, b in zip(held, got)]
            continue
        held = held + got
        if turn:
            taken, weights = weights[: len(held) * TIME_ORDERS], weights[len(held) * TIME_ORDERS :]
            held = [sum(taken[i * TIME_ORDERS + j] * a for i, a in enumerate(held)) for j in range(TIME_ORDERS)]


def freq_gather(state):
    size = lax.axis_size("freq")
    if size <= 4:
        return [state] + [exchange(state, "freq", distance) for distance in range(1, size)]
    distance = 1
    while distance < size:
        state = jnp.concatenate([state, exchange(state, "freq", distance)], axis=0)
        distance *= 2
    return [state]


def turn(gains):
    flat = gains.reshape(-1, gains.shape[-1])
    padded = jnp.concatenate([flat, jnp.zeros((LANES - flat.shape[0], flat.shape[1]), f32)], axis=0)
    return padded.T


def sum_rows(rows, model_ref, vis_ref, masked_ref, turned_ref):
    directions, receptors = model_ref.shape[0], model_ref.shape[3]
    turned = turned_ref[rows, :]
    near = [jnp.broadcast_to(turned[:, k : k + 1], (ROWS, LANES)) for k in range(2 * directions)]
    near_sum = [near[k] + near[directions + k] for k in range(directions)]
    near_gap = [near[directions + k] - near[k] for k in range(directions)]
    sums = [None] * (3 * directions)
    shared = [None] * directions

    def add(total, term):
        return term if total is None else total + term

    for block in range(receptors // LANES):
        columns = pl.ds(block * LANES, LANES)
        moved = []
        whole = by_imag = by_real = None
        for k in range(directions):
            model_real = model_ref[k, 0, rows, columns].astype(f32)
            model_imag = model_ref[k, 1, rows, columns].astype(f32)
            gain_real = masked_ref[0, k : k + 1, columns]
            gain_imag = masked_ref[1, k : k + 1, columns]
            real = model_real * gain_real + model_imag * gain_imag
            imag = model_imag * gain_real - model_real * gain_imag
            both = real + imag
            moved.append((real, imag, both))
            whole = add(whole, near[k] * both)
            by_imag = add(by_imag, imag * near_sum[k])
            by_real = add(by_real, real * near_gap[k])
        resid_real = vis_ref[0, rows, columns].astype(f32) - (whole - by_imag)
        resid_imag = vis_ref[1, rows, columns].astype(f32) - (whole + by_real)
        resid_sum = resid_imag + resid_real
        resid_gap = resid_imag - resid_real
        for k, (real, imag, both) in enumerate(moved):
            shared[k] = add(shared[k], resid_real * both)
            sums[k] = add(sums[k], imag * resid_gap)
            sums[directions + k] = add(sums[directions + k], real * resid_sum)
            sums[2 * directions + k] = add(sums[2 * directions + k], real * real + imag * imag)
    for k in range(directions):
        sums[k] = sums[k] + shared[k]
        sums[directions + k] = sums[directions + k] - shared[k]
    lane = lax.broadcasted_iota(jnp.int32, (ROWS, LANES), 1)
    out = jnp.zeros((ROWS, LANES), f32)
    for place, total in enumerate(sums):
        out = jnp.where(lane == place, jnp.sum(total, axis=1, keepdims=True), out)
    return out


def sum_range(start, count, unroll, sums_ref, model_ref, vis_ref, masked_ref, turned_ref, offset=0):
    def step(at, carry):
        first = pl.multiple_of(at * ROWS, ROWS)
        rows = pl.ds(pl.multiple_of(start + first, ROWS), ROWS)
        sums_ref[pl.ds(pl.multiple_of(offset + first, ROWS), ROWS), :] = sum_rows(rows, model_ref, vis_ref, masked_ref, turned_ref)
        return carry

    lax.fori_loop(0, count // ROWS, step, 0, unroll=unroll)


def part_kernel(start, unroll, model_ref, vis_ref, masked_ref, turned_ref, sums_ref):
    sum_range(start, sums_ref.shape[0], unroll, sums_ref, model_ref, vis_ref, masked_ref, turned_ref)


def begin_kernel(plan, chunks, unroll, gains_in, duals_in, flags_in, model_in, vis_in, *refs):
    gains_ref, merged_ref, masked_ref, turned_ref, mask_ref, model_ref, vis_ref, sums_ref = refs[:8]
    *weight_refs, duals_ref, flags_ref, sems = refs[8:]

    def copy(at, source, target):
        return pltpu.make_async_copy(source, target, sems.at[at])

    small = [copy(0, gains_in, gains_ref), copy(1, duals_in, duals_ref), copy(2, flags_in, flags_ref)]
    large = []
    for at, (first, length) in enumerate(chunks):
        rows = pl.ds(first, length)
        large.append(
            (
                copy(3 + 2 * at, model_in.at[:, :, rows, :], model_ref.at[:, :, rows, :]),
                copy(4 + 2 * at, vis_in.at[:, rows, :], vis_ref.at[:, rows, :]),
            )
        )
    for one in small:
        one.start()
    for pair in large:
        for one in pair:
            one.start()

    axis, size, distances = plan
    index = jnp.full((8, LANES), lax.axis_index(axis), jnp.int32)
    for ref, weight in zip(weight_refs, time_weights(size, distances, index)):
        ref[...] = jnp.broadcast_to(jnp.tile(weight, (ref.shape[1] // 8, ref.shape[2] // LANES))[None], ref.shape)

    for one in small:
        one.wait()
    gains = gains_ref[...]
    mask = flags_ref[...].astype(f32)
    mask_ref[...] = mask
    merged_ref[...] = gains + duals_ref[...]
    masked_ref[...] = gains * mask[None]
    turned_ref[...] = turn(gains)

    for (first, length), pair in zip(chunks, large):
        for one in pair:
            one.wait()
        if first < sums_ref.shape[0]:
            sum_range(first, length, unroll, sums_ref, model_ref, vis_ref, masked_ref, turned_ref, offset=first)


def transposed_sums(refs):
    return jnp.concatenate([ref[...] for ref in refs], axis=0).T


def projected(weight_refs, held_refs, got_ref):
    total = got_ref[...]
    for weight_ref, held_ref in zip(weight_refs, held_refs):
        total = total + weight_ref[...] * held_ref[...]
    return total


def middle_kernel(parts, terms, *refs):
    sums_refs, weight_refs, held_refs = refs[:parts], refs[parts : parts + terms], refs[parts + terms : parts + 2 * terms]
    got_ref, merged_ref, gains_ref, mask_ref, out_ref = refs[parts + 2 * terms :]
    sums = transposed_sums(sums_refs)
    mask = mask_ref[...]
    directions = gains_ref.shape[1]
    curvature = sums[2 * directions : 3 * directions] * mask
    inverse = 1.0 / (curvature + penalty)
    along_time = projected(weight_refs, held_refs, got_ref)
    for part in range(2):
        numer = sums[part * directions : (part + 1) * directions] * mask
        fixed = numer + curvature * gains_ref[part] - penalty * merged_ref[part]
        out_ref[0, part] = along_time[part]
        out_ref[0, 2 + part] = fixed * inverse
    out_ref[0, 4] = (2.0 * penalty) * inverse


def update_kernel(size, *refs):
    *gathered, merged_ref, mask_ref, gains_ref, duals_ref, along_ref, masked_ref, turned_ref = refs
    rows, lanes = merged_ref.shape[1:]
    index = lax.axis_index("freq")
    held, bases = [], []
    for ref in gathered:
        for at in range(ref.shape[0]):
            held.append((ref, at))
            place = jnp.full((8, LANES), index ^ (len(held) - 1), jnp.int32).astype(f32)
            basis = poly_basis(size, place, FREQ_ORDERS)
            bases.append([jnp.tile(weight, (rows // 8, lanes // LANES)) for weight in basis])
    gains, duals, along = [], [], []
    for part in range(2):
        values = [ref[at, part] for ref, at in held]
        coeffs = [sum(basis[i] * value for basis, value in zip(bases, values)) for i in range(FREQ_ORDERS)]
        solved = []
        for (ref, at), basis in zip(held, bases):
            consensus = sum(weight * coeff for weight, coeff in zip(basis, coeffs))
            if not solved:
                duals.append(merged_ref[part] - consensus)
            solved.append(ref[at, 2 + part] + ref[at, 4] * consensus)
        coeffs = [sum(basis[i] * value for basis, value in zip(bases, solved)) for i in range(FREQ_ORDERS)]
        gains.append(solved[0])
        along.append(sum(weight * coeff for weight, coeff in zip(bases[0], coeffs)))
    gains = jnp.stack(gains)
    gains_ref[...] = gains
    duals_ref[...] = jnp.stack(duals)
    along_ref[...] = jnp.stack(along)
    masked_ref[...] = gains * mask_ref[...][None]
    turned_ref[...] = turn(gains)


def finish_kernel(parts, terms, *refs):
    sums_refs, weight_refs, held_refs = refs[:parts], refs[parts : parts + terms], refs[parts + terms : parts + 2 * terms]
    got_ref, gains_ref, duals_ref, mask_ref, solved_ref, consensus_ref, final_ref = refs[parts + 2 * terms :]
    sums = transposed_sums(sums_refs)
    gains = gains_ref[...]
    mask = mask_ref[...]
    directions = gains.shape[1]
    consensus = projected(weight_refs, held_refs, got_ref)
    duals = duals_ref[...] + gains - consensus
    target = consensus - duals
    curvature = sums[2 * directions : 3 * directions] * mask
    divisor = curvature + penalty
    for part in range(2):
        numer = sums[part * directions : (part + 1) * directions] * mask
        solved_ref[part] = (numer + curvature * gains[part] + penalty * target[part]) / divisor
    consensus_ref[...] = consensus
    final_ref[...] = duals


def cut(total, shares):
    ends, done = [0], 0.0
    for share in shares:
        done += share
        ends.append(round(total * done / sum(shares)))
    return [(a, b - a) for a, b in zip(ends, ends[1:])]


def per_device(visibilities, model_vis, station_flags, initial_gains, initial_duals):
    vis_block = visibilities[0, 0]
    model_block = model_vis[0]
    flag_block = station_flags[0]
    _, directions, receptors = initial_gains.shape[2:]
    state = jax.ShapeDtypeStruct((2, directions, receptors), f32)
    turned_shape = jax.ShapeDtypeStruct((receptors, LANES), f32)
    pairs = directions * receptors

    freq_count, time_count = lax.axis_size("freq"), lax.axis_size("tm")
    distances = [1 << b for b in reversed(range(time_count.bit_length() - 1))]
    steps = len(distances)
    units = receptors // ROWS

    def sums_shape(length):
        return jax.ShapeDtypeStruct((length, LANES), f32)

    def cost(length):
        return pl.CostEstimate(flops=28 * pairs * length, bytes_accessed=4 * pairs * length, transcendentals=0)

    first, *beside = [(ROWS * a, ROWS * n) for a, n in cut(units, [11.0] + [9.0] * (steps - 1) + [4.0])]
    chunks = [(ROWS * a, ROWS * n) for a, n in cut(first[1] // ROWS, [1.0, 2.0, 2.0, 2.0]) if n]
    rest = receptors - first[1]
    chunks += [(first[1] + ROWS * a, ROWS * n) for a, n in cut(rest // ROWS, [1.0, 1.0])]
    gains, merged, masked, turned, mask, model_near, vis_near, sums, *weights = pl.pallas_call(
        functools.partial(begin_kernel, ("tm", time_count, distances), chunks, True),
        out_shape=[state] * 3
        + [
            turned_shape,
            jax.ShapeDtypeStruct((1, receptors), f32),
            jax.ShapeDtypeStruct(model_block.shape, model_block.dtype),
            jax.ShapeDtypeStruct(vis_block.shape, vis_block.dtype),
            sums_shape(first[1]),
        ]
        + [state] * time_weight_count(distances),
        in_specs=[pl.BlockSpec(memory_space=pltpu.HBM)] * 5,
        out_specs=whole_vmem(8 + time_weight_count(distances)),
        scratch_shapes=[
            pltpu.VMEM(state.shape, f32),
            pltpu.VMEM((1, receptors), jnp.int32),
            pltpu.SemaphoreType.DMA((3 + 2 * len(chunks),)),
        ],
        compiler_params=pltpu.CompilerParams(vmem_limit_bytes=32 * MIB),
        cost_estimate=cost(first[1]),
        name="begin",
    )(initial_gains[0, 0], initial_duals[0, 0], flag_block, model_block, vis_block)
    sums = [sums]

    def part(name, start, length, masked, turned):
        return pl.pallas_call(
            functools.partial(part_kernel, start, True),
            out_shape=sums_shape(length),
            in_specs=whole_vmem(4),
            out_specs=pl.BlockSpec(memory_space=pltpu.VMEM),
            compiler_params=pltpu.CompilerParams(vmem_limit_bytes=32 * MIB),
            cost_estimate=cost(length),
            name=name,
        )(model_near, vis_near, masked, turned)

    def worker(name, ranges, results, masked, turned):
        def work(at, message, distance):
            message, one, two = lax.optimization_barrier((message, masked, turned))
            got = exchange(message, "tm", distance)
            result = part(f"{name}{at}", *ranges[at], one, two)
            got, result = lax.optimization_barrier((got, result))
            results.append(result)
            return got

        return work

    def small_kernel(kernel, name, operands, outs):
        return pl.pallas_call(
            kernel,
            out_shape=outs,
            in_specs=whole_vmem(len(operands)),
            out_specs=whole_vmem(len(outs)),
            compiler_params=pltpu.CompilerParams(vmem_limit_bytes=16 * MIB),
            name=name,
        )(*operands)

    held, own, got = time_exchange(merged, distances, weights, worker("first", beside, sums, masked, turned))
    operands = sums + own + held + [got, merged, gains, mask]
    (payload,) = small_kernel(
        functools.partial(middle_kernel, len(sums), len(held)),
        "middle",
        operands,
        [jax.ShapeDtypeStruct((1, 5, directions, receptors), f32)],
    )
    gathered = freq_gather(payload)
    gains, duals, along_freq, masked, turned = small_kernel(
        functools.partial(update_kernel, freq_count),
        "update",
        gathered + [merged, mask],
        [state] * 4 + [turned_shape],
    )

    beside = [(ROWS * a, ROWS * n) for a, n in cut(units, [11.0] * (steps - 1) + [10.0])]
    sums = []
    held, own, got = time_exchange(along_freq, distances, weights, worker("second", beside, sums, masked, turned))
    operands = sums + own + held + [got, gains, duals, mask]
    outputs = small_kernel(functools.partial(finish_kernel, len(sums), len(held)), "finish", operands, [state] * 3)
    return tuple(out[None, None] for out in outputs)


def solution(mesh):
    in_specs = (
        P("freq", "tm", None, None, None),
        P("freq", None, None, None, None),
        P("freq", "tm", None),
        P("freq", "tm", None, None, None),
        P("freq", "tm", None, None, None),
    )
    out_specs = (
        P("freq", "tm", None, None, None),
        P("freq", "tm", None, None, None),
        P("freq", "tm", None, None, None),
    )
    return jax.shard_map(
        per_device, mesh=mesh, in_specs=in_specs, out_specs=out_specs, check_vma=False
    )
```

```python
import functools
import math

import jax
import jax.numpy as jnp
from jax import lax
from jax.experimental import pallas as pl
from jax.experimental.pallas import tpu as pltpu
from jax.sharding import PartitionSpec as P

LANES = 128
ROWS = 16
FREQ_ORDERS = 3
TIME_ORDERS = 2
MIB = 2**20

penalty = 1.0
f32 = jnp.float32


def poly_basis(length, position, order_count):
    centre = position - (length - 1) / 2.0
    linear = centre * (1.0 / math.sqrt(length * (length * length - 1) / 12.0))
    stacked = [jnp.ones_like(position) * (1.0 / math.sqrt(length)), linear]
    if order_count == 3:
        scale = math.sqrt(length * (length * length - 1) * (length * length - 4) / 180.0)
        stacked.append((centre * centre - (length * length - 1) / 12.0) * (1.0 / scale))
    return stacked


def whole_vmem(count):
    return [pl.BlockSpec(memory_space=pltpu.VMEM)] * count


def exchange(array, axis, distance):
    size = lax.axis_size(axis)
    return lax.ppermute(array, axis, [(place, place ^ distance) for place in range(size)])


def time_plan(distances):
    steps = []
    held, sums = 1, False
    for at in range(len(distances)):
        last = at == len(distances) - 1
        turn = not last and not sums and 2 * held > TIME_ORDERS and at < len(distances) - 2
        steps.append((held, sums, turn))
        if turn:
            held, sums = TIME_ORDERS, True
        elif not sums:
            held = 2 * held
    return steps


def time_weights(size, distances, index):
    weights = []

    def basis(place):
        return poly_basis(size, lax.convert_element_type(place, f32), TIME_ORDERS)

    def product(one, other):
        return sum(a * b for a, b in zip(basis(one), basis(other)))

    raw = [index]
    for at, (held, sums, turn) in enumerate(time_plan(distances)):
        if at == len(distances) - 1:
            for target in (index ^ distances[at], index):
                weights += basis(target) if sums else [product(target, place) for place in raw]
        elif not sums:
            raw = raw + [place ^ distances[at] for place in raw]
            if turn:
                for place in raw:
                    weights += basis(place)
    return weights


def time_weight_count(distances):
    total, raw = 0, 1
    for at, (held, sums, turn) in enumerate(time_plan(distances)):
        if at == len(distances) - 1:
            total += 2 * held
        elif not sums:
            raw = 2 * raw
            total += raw * TIME_ORDERS if turn else 0
    return total


def time_exchange(state, distances, weights, work):
    weights = list(weights)
    held = [state]
    for at, (_, sums, turn) in enumerate(time_plan(distances)):
        if at == len(distances) - 1:
            away, own = weights[: len(held)], weights[len(held) :]
            got = work(at, sum(w * a for w, a in zip(away, held)), distances[at])
            return held, own, got
        message = held[0] if len(held) == 1 else jnp.stack(held)
        got = work(at, message, distances[at])
        got = [got] if len(held) == 1 else [got[i] for i in range(len(held))]
        if sums:
            held = [a + b for a, b in zip(held, got)]
            continue
        held = held + got
        if turn:
            taken, weights = weights[: len(held) * TIME_ORDERS], weights[len(held) * TIME_ORDERS :]
            held = [sum(taken[i * TIME_ORDERS + j] * a for i, a in enumerate(held)) for j in range(TIME_ORDERS)]


def freq_gather(state):
    size = lax.axis_size("freq")
    if size <= 4:
        return [state] + [exchange(state, "freq", distance) for distance in range(1, size)]
    distance = 1
    while distance < size:
        state = jnp.concatenate([state, exchange(state, "freq", distance)], axis=0)
        distance *= 2
    return [state]


def turn(gains):
    flat = gains.reshape(-1, gains.shape[-1])
    padded = jnp.concatenate([flat, jnp.zeros((LANES - flat.shape[0], flat.shape[1]), f32)], axis=0)
    return padded.T


def sum_rows(rows, model_ref, vis_ref, masked_ref, turned_ref):
    directions, receptors = model_ref.shape[0], model_ref.shape[3]
    turned = turned_ref[rows, :]
    near = [jnp.broadcast_to(turned[:, k : k + 1], (ROWS, LANES)) for k in range(2 * directions)]
    near_sum = [near[k] + near[directions + k] for k in range(directions)]
    near_gap = [near[directions + k] - near[k] for k in range(directions)]
    sums = [None] * (3 * directions)
    shared = [None] * directions

    def add(total, term):
        return term if total is None else total + term

    for block in range(receptors // LANES):
        columns = pl.ds(block * LANES, LANES)
        moved = []
        whole = by_imag = by_real = None
        for k in range(directions):
            model_real = model_ref[k, 0, rows, columns].astype(f32)
            model_imag = model_ref[k, 1, rows, columns].astype(f32)
            gain_real = masked_ref[0, k : k + 1, columns]
            gain_imag = masked_ref[1, k : k + 1, columns]
            real = model_real * gain_real + model_imag * gain_imag
            imag = model_imag * gain_real - model_real * gain_imag
            both = real + imag
            moved.append((real, imag, both))
            whole = add(whole, near[k] * both)
            by_imag = add(by_imag, imag * near_sum[k])
            by_real = add(by_real, real * near_gap[k])
        resid_real = vis_ref[0, rows, columns].astype(f32) - (whole - by_imag)
        resid_imag = vis_ref[1, rows, columns].astype(f32) - (whole + by_real)
        resid_sum = resid_imag + resid_real
        resid_gap = resid_imag - resid_real
        for k, (real, imag, both) in enumerate(moved):
            shared[k] = add(shared[k], resid_real * both)
            sums[k] = add(sums[k], imag * resid_gap)
            sums[directions + k] = add(sums[directions + k], real * resid_sum)
            sums[2 * directions + k] = add(sums[2 * directions + k], real * real + imag * imag)
    for k in range(directions):
        sums[k] = sums[k] + shared[k]
        sums[directions + k] = sums[directions + k] - shared[k]
    lane = lax.broadcasted_iota(jnp.int32, (ROWS, LANES), 1)
    out = jnp.zeros((ROWS, LANES), f32)
    for place, total in enumerate(sums):
        out = jnp.where(lane == place, jnp.sum(total, axis=1, keepdims=True), out)
    return out


def sum_range(start, count, unroll, sums_ref, model_ref, vis_ref, masked_ref, turned_ref, offset=0):
    def step(at, carry):
        first = pl.multiple_of(at * ROWS, ROWS)
        rows = pl.ds(pl.multiple_of(start + first, ROWS), ROWS)
        sums_ref[pl.ds(pl.multiple_of(offset + first, ROWS), ROWS), :] = sum_rows(rows, model_ref, vis_ref, masked_ref, turned_ref)
        return carry

    lax.fori_loop(0, count // ROWS, step, 0, unroll=unroll)


def part_kernel(start, unroll, model_ref, vis_ref, masked_ref, turned_ref, sums_ref):
    sum_range(start, sums_ref.shape[0], unroll, sums_ref, model_ref, vis_ref, masked_ref, turned_ref)


def setup_kernel(plan, gains_in, duals_in, flags_in, gains_ref, merged_ref, masked_ref, turned_ref, mask_ref, *refs):
    *weight_refs, duals_ref, flags_ref, sems = refs
    places = ((gains_in, gains_ref), (duals_in, duals_ref), (flags_in, flags_ref))
    copies = [pltpu.make_async_copy(source, target, sems.at[at]) for at, (source, target) in enumerate(places)]
    for copy in copies:
        copy.start()
    axis, size, distances = plan
    index = jnp.full((8, LANES), lax.axis_index(axis), jnp.int32)
    for ref, weight in zip(weight_refs, time_weights(size, distances, index)):
        ref[...] = jnp.broadcast_to(jnp.tile(weight, (ref.shape[1] // 8, ref.shape[2] // LANES))[None], ref.shape)
    for copy in copies:
        copy.wait()
    gains = gains_ref[...]
    mask = flags_ref[...].astype(f32)
    mask_ref[...] = mask
    merged_ref[...] = gains + duals_ref[...]
    masked_ref[...] = gains * mask[None]
    turned_ref[...] = turn(gains)


def transposed_sums(refs):
    return jnp.concatenate([ref[...] for ref in refs], axis=0).T


def projected(weight_refs, held_refs, got_ref):
    total = got_ref[...]
    for weight_ref, held_ref in zip(weight_refs, held_refs):
        total = total + weight_ref[...] * held_ref[...]
    return total


def middle_kernel(parts, terms, *refs):
    sums_refs, weight_refs, held_refs = refs[:parts], refs[parts : parts + terms], refs[parts + terms : parts + 2 * terms]
    got_ref, merged_ref, gains_ref, mask_ref, out_ref = refs[parts + 2 * terms :]
    sums = transposed_sums(sums_refs)
    mask = mask_ref[...]
    directions = gains_ref.shape[1]
    curvature = sums[2 * directions : 3 * directions] * mask
    inverse = 1.0 / (curvature + penalty)
    along_time = projected(weight_refs, held_refs, got_ref)
    for part in range(2):
        numer = sums[part * directions : (part + 1) * directions] * mask
        fixed = numer + curvature * gains_ref[part] - penalty * merged_ref[part]
        out_ref[0, part] = along_time[part]
        out_ref[0, 2 + part] = fixed * inverse
    out_ref[0, 4] = (2.0 * penalty) * inverse


def update_kernel(size, *refs):
    *gathered, merged_ref, mask_ref, gains_ref, duals_ref, along_ref, masked_ref, turned_ref = refs
    rows, lanes = merged_ref.shape[1:]
    index = lax.axis_index("freq")
    held, bases = [], []
    for ref in gathered:
        for at in range(ref.shape[0]):
            held.append((ref, at))
            place = jnp.full((8, LANES), index ^ (len(held) - 1), jnp.int32).astype(f32)
            basis = poly_basis(size, place, FREQ_ORDERS)
            bases.append([jnp.tile(weight, (rows // 8, lanes // LANES)) for weight in basis])
    gains, duals, along = [], [], []
    for part in range(2):
        values = [ref[at, part] for ref, at in held]
        coeffs = [sum(basis[i] * value for basis, value in zip(bases, values)) for i in range(FREQ_ORDERS)]
        solved = []
        for (ref, at), basis in zip(held, bases):
            consensus = sum(weight * coeff for weight, coeff in zip(basis, coeffs))
            if not solved:
                duals.append(merged_ref[part] - consensus)
            solved.append(ref[at, 2 + part] + ref[at, 4] * consensus)
        coeffs = [sum(basis[i] * value for basis, value in zip(bases, solved)) for i in range(FREQ_ORDERS)]
        gains.append(solved[0])
        along.append(sum(weight * coeff for weight, coeff in zip(bases[0], coeffs)))
    gains = jnp.stack(gains)
    gains_ref[...] = gains
    duals_ref[...] = jnp.stack(duals)
    along_ref[...] = jnp.stack(along)
    masked_ref[...] = gains * mask_ref[...][None]
    turned_ref[...] = turn(gains)


def finish_kernel(parts, terms, *refs):
    sums_refs, weight_refs, held_refs = refs[:parts], refs[parts : parts + terms], refs[parts + terms : parts + 2 * terms]
    got_ref, gains_ref, duals_ref, mask_ref, solved_ref, consensus_ref, final_ref = refs[parts + 2 * terms :]
    sums = transposed_sums(sums_refs)
    gains = gains_ref[...]
    mask = mask_ref[...]
    directions = gains.shape[1]
    consensus = projected(weight_refs, held_refs, got_ref)
    duals = duals_ref[...] + gains - consensus
    target = consensus - duals
    curvature = sums[2 * directions : 3 * directions] * mask
    divisor = curvature + penalty
    for part in range(2):
        numer = sums[part * directions : (part + 1) * directions] * mask
        solved_ref[part] = (numer + curvature * gains[part] + penalty * target[part]) / divisor
    consensus_ref[...] = consensus
    final_ref[...] = duals


def cut(total, shares):
    ends, done = [0], 0.0
    for share in shares:
        done += share
        ends.append(round(total * done / sum(shares)))
    return [(a, b - a) for a, b in zip(ends, ends[1:])]


def per_device(visibilities, model_vis, station_flags, initial_gains, initial_duals):
    vis_block = visibilities[0, 0]
    model_block = model_vis[0]
    _, directions, receptors = initial_gains.shape[2:]
    state = jax.ShapeDtypeStruct((2, directions, receptors), f32)
    turned_shape = jax.ShapeDtypeStruct((receptors, LANES), f32)
    pairs = directions * receptors

    freq_count, time_count = lax.axis_size("freq"), lax.axis_size("tm")
    distances = [1 << b for b in reversed(range(time_count.bit_length() - 1))]
    steps = len(distances)
    units = receptors // ROWS

    def sums_shape(length):
        return jax.ShapeDtypeStruct((length, LANES), f32)

    def cost(length):
        return pl.CostEstimate(flops=28 * pairs * length, bytes_accessed=4 * pairs * length, transcendentals=0)

    small = [initial_gains[0, 0], initial_duals[0, 0], station_flags[0]]
    gains, merged, masked, turned, mask, *weights = pl.pallas_call(
        functools.partial(setup_kernel, ("tm", time_count, distances)),
        out_shape=[state] * 3
        + [turned_shape, jax.ShapeDtypeStruct((1, receptors), f32)]
        + [state] * time_weight_count(distances),
        in_specs=[pl.BlockSpec(memory_space=pltpu.HBM)] * 3,
        out_specs=whole_vmem(5 + time_weight_count(distances)),
        scratch_shapes=[
            pltpu.VMEM(state.shape, f32),
            pltpu.VMEM((1, receptors), jnp.int32),
            pltpu.SemaphoreType.DMA((3,)),
        ],
        compiler_params=pltpu.CompilerParams(vmem_limit_bytes=16 * MIB),
        cost_estimate=pl.CostEstimate(flops=1 << 36, bytes_accessed=1 << 28, transcendentals=0),
        name="setup",
    )(*[pltpu.with_memory_space_constraint(one, pltpu.HBM) for one in small])

    def part(name, start, length, masked, turned):
        return pl.pallas_call(
            functools.partial(part_kernel, start, True),
            out_shape=sums_shape(length),
            in_specs=whole_vmem(4),
            out_specs=pl.BlockSpec(memory_space=pltpu.VMEM),
            compiler_params=pltpu.CompilerParams(vmem_limit_bytes=32 * MIB),
            cost_estimate=cost(length),
            name=name,
        )(model_block, vis_block, masked, turned)

    def worker(name, ranges, results, masked, turned):
        def work(at, message, distance):
            message, one, two = lax.optimization_barrier((message, masked, turned))
            got = exchange(message, "tm", distance)
            result = part(f"{name}{at}", *ranges[at], one, two)
            got, result = lax.optimization_barrier((got, result))
            results.append(result)
            return got

        return work

    def small_kernel(kernel, name, operands, outs):
        return pl.pallas_call(
            kernel,
            out_shape=outs,
            in_specs=whole_vmem(len(operands)),
            out_specs=whole_vmem(len(outs)),
            compiler_params=pltpu.CompilerParams(vmem_limit_bytes=16 * MIB),
            name=name,
        )(*operands)

    beside = [(ROWS * a, ROWS * n) for a, n in cut(units, [11.0] * (steps - 1) + [10.0])]
    sums = []
    held, own, got = time_exchange(merged, distances, weights, worker("first", beside, sums, masked, turned))
    operands = sums + own + held + [got, merged, gains, mask]
    (payload,) = small_kernel(
        functools.partial(middle_kernel, len(sums), len(held)),
        "middle",
        operands,
        [jax.ShapeDtypeStruct((1, 5, directions, receptors), f32)],
    )
    gathered = freq_gather(payload)
    gains, duals, along_freq, masked, turned = small_kernel(
        functools.partial(update_kernel, freq_count),
        "update",
        gathered + [merged, mask],
        [state] * 4 + [turned_shape],
    )

    sums = []
    held, own, got = time_exchange(along_freq, distances, weights, worker("second", beside, sums, masked, turned))
    operands = sums + own + held + [got, gains, duals, mask]
    outputs = small_kernel(functools.partial(finish_kernel, len(sums), len(held)), "finish", operands, [state] * 3)
    return tuple(out[None, None] for out in outputs)


def solution(mesh):
    in_specs = (
        P("freq", "tm", None, None, None),
        P("freq", None, None, None, None),
        P("freq", "tm", None),
        P("freq", "tm", None, None, None),
        P("freq", "tm", None, None, None),
    )
    out_specs = (
        P("freq", "tm", None, None, None),
        P("freq", "tm", None, None, None),
        P("freq", "tm", None, None, None),
    )
    return jax.shard_map(
        per_device, mesh=mesh, in_specs=in_specs, out_specs=out_specs, check_vma=False
    )
```

```python
import functools
import math

import jax
import jax.numpy as jnp
from jax import lax
from jax.experimental import pallas as pl
from jax.experimental.pallas import tpu as pltpu
from jax.sharding import PartitionSpec as P

LANES = 128
ROWS = 16
FREQ_ORDERS = 3
TIME_ORDERS = 2
MIB = 2**20

penalty = 1.0
f32 = jnp.float32


def poly_basis(length, position, order_count):
    centre = position - (length - 1) / 2.0
    linear = centre * (1.0 / math.sqrt(length * (length * length - 1) / 12.0))
    stacked = [jnp.ones_like(position) * (1.0 / math.sqrt(length)), linear]
    if order_count == 3:
        scale = math.sqrt(length * (length * length - 1) * (length * length - 4) / 180.0)
        stacked.append((centre * centre - (length * length - 1) / 12.0) * (1.0 / scale))
    return stacked


def whole_vmem(count):
    return [pl.BlockSpec(memory_space=pltpu.VMEM)] * count


def exchange(array, axis, distance):
    size = lax.axis_size(axis)
    return lax.ppermute(array, axis, [(place, place ^ distance) for place in range(size)])


def time_plan(distances):
    steps = []
    held, sums = 1, False
    for at in range(len(distances)):
        last = at == len(distances) - 1
        turn = not last and not sums and 2 * held > TIME_ORDERS and at < len(distances) - 2
        steps.append((held, sums, turn))
        if turn:
            held, sums = TIME_ORDERS, True
        elif not sums:
            held = 2 * held
    return steps


def time_weights(size, distances, index):
    weights = []

    def basis(place):
        return poly_basis(size, lax.convert_element_type(place, f32), TIME_ORDERS)

    def product(one, other):
        return sum(a * b for a, b in zip(basis(one), basis(other)))

    raw = [index]
    for at, (held, sums, turn) in enumerate(time_plan(distances)):
        if at == len(distances) - 1:
            for target in (index ^ distances[at], index):
                weights += basis(target) if sums else [product(target, place) for place in raw]
        elif not sums:
            raw = raw + [place ^ distances[at] for place in raw]
            if turn:
                for place in raw:
                    weights += basis(place)
    return weights


def time_weight_count(distances):
    total, raw = 0, 1
    for at, (held, sums, turn) in enumerate(time_plan(distances)):
        if at == len(distances) - 1:
            total += 2 * held
        elif not sums:
            raw = 2 * raw
            total += raw * TIME_ORDERS if turn else 0
    return total


def time_exchange(state, distances, weights, work):
    weights = list(weights)
    held = [state]
    for at, (_, sums, turn) in enumerate(time_plan(distances)):
        if at == len(distances) - 1:
            away, own = weights[: len(held)], weights[len(held) :]
            got = work(at, sum(w * a for w, a in zip(away, held)), distances[at])
            return held, own, got
        message = held[0] if len(held) == 1 else jnp.stack(held)
        got = work(at, message, distances[at])
        got = [got] if len(held) == 1 else [got[i] for i in range(len(held))]
        if sums:
            held = [a + b for a, b in zip(held, got)]
            continue
        held = held + got
        if turn:
            taken, weights = weights[: len(held) * TIME_ORDERS], weights[len(held) * TIME_ORDERS :]
            held = [sum(taken[i * TIME_ORDERS + j] * a for i, a in enumerate(held)) for j in range(TIME_ORDERS)]


def freq_gather(state):
    size = lax.axis_size("freq")
    if size <= 4:
        return [state] + [exchange(state, "freq", distance) for distance in range(1, size)]
    distance = 1
    while distance < size:
        state = jnp.concatenate([state, exchange(state, "freq", distance)], axis=0)
        distance *= 2
    return [state]


def turn(gains):
    flat = gains.reshape(-1, gains.shape[-1])
    padded = jnp.concatenate([flat, jnp.zeros((LANES - flat.shape[0], flat.shape[1]), f32)], axis=0)
    return padded.T


def sum_rows(rows, model_ref, vis_ref, masked_ref, turned_ref, square_ref=None, power_ref=None):
    directions, blocks = model_ref.shape[0], model_ref.shape[3] // LANES
    turned = turned_ref[rows, :]

    def along_lanes(column):
        return jnp.take_along_axis(turned, jnp.full((ROWS, LANES), column, jnp.int32), axis=1)

    def add(total, term):
        return term if total is None else total + term

    whole, by_imag, by_real = [None] * blocks, [None] * blocks, [None] * blocks
    moved = {}
    for k in range(directions):
        near_real, near_imag = along_lanes(k), along_lanes(directions + k)
        near_sum, near_gap = near_real + near_imag, near_imag - near_real
        for block in range(blocks):
            columns = pl.ds(block * LANES, LANES)
            model_real = model_ref[k, 0, rows, columns].astype(f32)
            model_imag = model_ref[k, 1, rows, columns].astype(f32)
            gain_real = masked_ref[0, k : k + 1, columns]
            gain_imag = masked_ref[1, k : k + 1, columns]
            real = model_real * gain_real + model_imag * gain_imag
            imag = model_imag * gain_real - model_real * gain_imag
            both = real + imag
            moved[k, block] = (real, imag, both)
            whole[block] = add(whole[block], near_real * both)
            by_imag[block] = add(by_imag[block], imag * near_sum)
            by_real[block] = add(by_real[block], real * near_gap)
    residuals = []
    for block in range(blocks):
        columns = pl.ds(block * LANES, LANES)
        real = vis_ref[0, rows, columns].astype(f32) - (whole[block] - by_imag[block])
        imag = vis_ref[1, rows, columns].astype(f32) - (whole[block] + by_real[block])
        residuals.append((real, imag + real, imag - real))
    lane = lax.broadcasted_iota(jnp.int32, (ROWS, LANES), 1)
    out = jnp.zeros((ROWS, LANES), f32)
    for k in range(directions):
        shared = by_gap = by_sum = curvature = None
        for block in range(blocks):
            columns = pl.ds(block * LANES, LANES)
            real, imag, both = moved[k, block]
            resid_real, resid_sum, resid_gap = residuals[block]
            shared = add(shared, resid_real * both)
            by_gap = add(by_gap, imag * resid_gap)
            by_sum = add(by_sum, real * resid_sum)
            if square_ref is None:
                curvature = add(curvature, real * real + imag * imag)
            else:
                curvature = add(curvature, square_ref[k, rows, columns] * power_ref[k : k + 1, columns])
        for kind, total in enumerate((by_gap + shared, by_sum - shared, curvature)):
            out = jnp.where(lane == kind * directions + k, jnp.sum(total, axis=1, keepdims=True), out)
    return out


def part_kernel(start, unroll, *refs):
    *inputs, sums_ref = refs

    def step(at, carry):
        first = pl.multiple_of(at * ROWS, ROWS)
        rows = pl.ds(pl.multiple_of(start + first, ROWS), ROWS)
        sums_ref[pl.ds(first, ROWS), :] = sum_rows(rows, *inputs)
        return carry

    lax.fori_loop(0, sums_ref.shape[0] // ROWS, step, 0, unroll=unroll)


def widen_kernel(model_ref, wide_ref, square_ref):
    def step(at, carry):
        rows = pl.ds(pl.multiple_of(at * ROWS, ROWS), ROWS)
        for k in range(model_ref.shape[0]):
            real, imag = model_ref[k, 0, rows, :].astype(f32), model_ref[k, 1, rows, :].astype(f32)
            wide_ref[k, 0, rows, :] = real
            wide_ref[k, 1, rows, :] = imag
            square_ref[k, rows, :] = real * real + imag * imag
        return carry

    lax.fori_loop(0, model_ref.shape[2] // ROWS, step, 0, unroll=2)


def setup_kernel(plan, gains_in, duals_in, flags_in, gains_ref, merged_ref, masked_ref, turned_ref, mask_ref, *refs):
    *weight_refs, duals_ref, flags_ref, sems = refs
    places = ((gains_in, gains_ref), (duals_in, duals_ref), (flags_in, flags_ref))
    copies = [pltpu.make_async_copy(source, target, sems.at[at]) for at, (source, target) in enumerate(places)]
    for copy in copies:
        copy.start()
    axis, size, distances = plan
    index = jnp.full((8, LANES), lax.axis_index(axis), jnp.int32)
    for ref, weight in zip(weight_refs, time_weights(size, distances, index)):
        ref[...] = jnp.broadcast_to(jnp.tile(weight, (ref.shape[1] // 8, ref.shape[2] // LANES))[None], ref.shape)
    for copy in copies:
        copy.wait()
    gains = gains_ref[...]
    mask = flags_ref[...].astype(f32)
    mask_ref[...] = mask
    merged_ref[...] = gains + duals_ref[...]
    masked_ref[...] = gains * mask[None]
    turned_ref[...] = turn(gains)


def transposed_sums(refs):
    return jnp.concatenate([ref[...] for ref in refs], axis=0).T


def projected(weight_refs, held_refs, got_ref):
    total = got_ref[...]
    for weight_ref, held_ref in zip(weight_refs, held_refs):
        total = total + weight_ref[...] * held_ref[...]
    return total


def middle_kernel(parts, terms, *refs):
    sums_refs, weight_refs, held_refs = refs[:parts], refs[parts : parts + terms], refs[parts + terms : parts + 2 * terms]
    got_ref, merged_ref, gains_ref, mask_ref, out_ref = refs[parts + 2 * terms :]
    sums = transposed_sums(sums_refs)
    mask = mask_ref[...]
    directions = gains_ref.shape[1]
    curvature = sums[2 * directions : 3 * directions] * mask
    inverse = 1.0 / (curvature + penalty)
    along_time = projected(weight_refs, held_refs, got_ref)
    for part in range(2):
        numer = sums[part * directions : (part + 1) * directions] * mask
        fixed = numer + curvature * gains_ref[part] - penalty * merged_ref[part]
        out_ref[0, part] = along_time[part]
        out_ref[0, 2 + part] = fixed * inverse
    out_ref[0, 4] = (2.0 * penalty) * inverse


def update_kernel(size, *refs):
    *gathered, merged_ref, mask_ref, gains_ref, duals_ref, along_ref, masked_ref, turned_ref, power_ref = refs
    rows, lanes = merged_ref.shape[1:]
    index = lax.axis_index("freq")
    held, bases = [], []
    for ref in gathered:
        for at in range(ref.shape[0]):
            held.append((ref, at))
            place = jnp.full((8, LANES), index ^ (len(held) - 1), jnp.int32).astype(f32)
            basis = poly_basis(size, place, FREQ_ORDERS)
            bases.append([jnp.tile(weight, (rows // 8, lanes // LANES)) for weight in basis])
    gains, duals, along = [], [], []
    for part in range(2):
        values = [ref[at, part] for ref, at in held]
        coeffs = [sum(basis[i] * value for basis, value in zip(bases, values)) for i in range(FREQ_ORDERS)]
        solved = []
        for (ref, at), basis in zip(held, bases):
            consensus = sum(weight * coeff for weight, coeff in zip(basis, coeffs))
            if not solved:
                duals.append(merged_ref[part] - consensus)
            solved.append(ref[at, 2 + part] + ref[at, 4] * consensus)
        coeffs = [sum(basis[i] * value for basis, value in zip(bases, solved)) for i in range(FREQ_ORDERS)]
        gains.append(solved[0])
        along.append(sum(weight * coeff for weight, coeff in zip(bases[0], coeffs)))
    gains = jnp.stack(gains)
    gains_ref[...] = gains
    duals_ref[...] = jnp.stack(duals)
    along_ref[...] = jnp.stack(along)
    masked = gains * mask_ref[...][None]
    masked_ref[...] = masked
    turned_ref[...] = turn(gains)
    power_ref[...] = masked[0] * masked[0] + masked[1] * masked[1]


def finish_kernel(parts, terms, *refs):
    sums_refs, weight_refs, held_refs = refs[:parts], refs[parts : parts + terms], refs[parts + terms : parts + 2 * terms]
    got_ref, gains_ref, duals_ref, mask_ref, solved_ref, consensus_ref, final_ref = refs[parts + 2 * terms :]
    sums = transposed_sums(sums_refs)
    gains = gains_ref[...]
    mask = mask_ref[...]
    directions = gains.shape[1]
    consensus = projected(weight_refs, held_refs, got_ref)
    duals = duals_ref[...] + gains - consensus
    target = consensus - duals
    curvature = sums[2 * directions : 3 * directions] * mask
    divisor = curvature + penalty
    for part in range(2):
        numer = sums[part * directions : (part + 1) * directions] * mask
        solved_ref[part] = (numer + curvature * gains[part] + penalty * target[part]) / divisor
    consensus_ref[...] = consensus
    final_ref[...] = duals


def cut(total, shares):
    ends, done = [0], 0.0
    for share in shares:
        done += share
        ends.append(round(total * done / sum(shares)))
    return [(a, b - a) for a, b in zip(ends, ends[1:])]


def per_device(visibilities, model_vis, station_flags, initial_gains, initial_duals):
    vis_block = visibilities[0, 0]
    model_block = model_vis[0]
    _, directions, receptors = initial_gains.shape[2:]
    state = jax.ShapeDtypeStruct((2, directions, receptors), f32)
    turned_shape = jax.ShapeDtypeStruct((receptors, LANES), f32)
    pairs = directions * receptors

    freq_count, time_count = lax.axis_size("freq"), lax.axis_size("tm")
    distances = [1 << b for b in reversed(range(time_count.bit_length() - 1))]
    steps = len(distances)
    units = receptors // ROWS

    def sums_shape(length):
        return jax.ShapeDtypeStruct((length, LANES), f32)

    def cost(length):
        return pl.CostEstimate(flops=28 * pairs * length, bytes_accessed=4 * pairs * length, transcendentals=0)

    small = [initial_gains[0, 0], initial_duals[0, 0], station_flags[0]]
    gains, merged, masked, turned, mask, *weights = pl.pallas_call(
        functools.partial(setup_kernel, ("tm", time_count, distances)),
        out_shape=[state] * 3
        + [turned_shape, jax.ShapeDtypeStruct((1, receptors), f32)]
        + [state] * time_weight_count(distances),
        in_specs=[pl.BlockSpec(memory_space=pltpu.HBM)] * 3,
        out_specs=whole_vmem(5 + time_weight_count(distances)),
        scratch_shapes=[
            pltpu.VMEM(state.shape, f32),
            pltpu.VMEM((1, receptors), jnp.int32),
            pltpu.SemaphoreType.DMA((3,)),
        ],
        compiler_params=pltpu.CompilerParams(vmem_limit_bytes=4 * MIB),
        cost_estimate=pl.CostEstimate(flops=1 << 36, bytes_accessed=1 << 28, transcendentals=0),
        name="setup",
    )(*[pltpu.with_memory_space_constraint(one, pltpu.HBM) for one in small])

    def part(name, start, length, operands):
        return pl.pallas_call(
            functools.partial(part_kernel, start, True),
            out_shape=sums_shape(length),
            in_specs=whole_vmem(len(operands)),
            out_specs=pl.BlockSpec(memory_space=pltpu.VMEM),
            compiler_params=pltpu.CompilerParams(vmem_limit_bytes=3 * MIB),
            cost_estimate=cost(length),
            name=name,
        )(*operands)

    def worker(name, ranges, results, fixed, now):
        def work(at, message, distance):
            message, current = lax.optimization_barrier((message, now))
            got = exchange(message, "tm", distance)
            result = part(f"{name}{at}", *ranges[at], fixed[:2] + current[:2] + fixed[2:] + current[2:])
            got, result = lax.optimization_barrier((got, result))
            results.append(result)
            return got

        return work

    def small_kernel(kernel, name, operands, outs):
        return pl.pallas_call(
            kernel,
            out_shape=outs,
            in_specs=whole_vmem(len(operands)),
            out_specs=whole_vmem(len(outs)),
            compiler_params=pltpu.CompilerParams(vmem_limit_bytes=4 * MIB),
            name=name,
        )(*operands)

    beside = [(ROWS * a, ROWS * n) for a, n in cut(units, [13.0] * (steps - 1) + [6.0])]
    sums = []
    held, own, got = time_exchange(merged, distances, weights, worker("first", beside, sums, [model_block, vis_block], [masked, turned]))
    operands = sums + own + held + [got, merged, gains, mask]
    (payload,) = small_kernel(
        functools.partial(middle_kernel, len(sums), len(held)),
        "middle",
        operands,
        [jax.ShapeDtypeStruct((1, 5, directions, receptors), f32)],
    )
    payload, model_now = lax.optimization_barrier((payload, model_block))
    gathered = freq_gather(payload)
    model_wide, model_square = pl.pallas_call(
        widen_kernel,
        out_shape=[
            jax.ShapeDtypeStruct(model_block.shape, f32),
            jax.ShapeDtypeStruct((directions, receptors, receptors), f32),
        ],
        in_specs=whole_vmem(1),
        out_specs=whole_vmem(2),
        compiler_params=pltpu.CompilerParams(vmem_limit_bytes=3 * MIB),
        cost_estimate=pl.CostEstimate(flops=28 * pairs * 96, bytes_accessed=12 * pairs * receptors, transcendentals=0),
        name="widen",
    )(model_now)
    gathered, model_wide, model_square = lax.optimization_barrier((gathered, model_wide, model_square))
    gains, duals, along_freq, masked, turned, power = small_kernel(
        functools.partial(update_kernel, freq_count),
        "update",
        gathered + [merged, mask],
        [state] * 4 + [turned_shape, jax.ShapeDtypeStruct((directions, receptors), f32)],
    )

    sums = []
    held, own, got = time_exchange(along_freq, distances, weights, worker("second", beside, sums, [model_wide, vis_block, model_square], [masked, turned, power]))
    operands = sums + own + held + [got, gains, duals, mask]
    outputs = small_kernel(functools.partial(finish_kernel, len(sums), len(held)), "finish", operands, [state] * 3)
    return tuple(out[None, None] for out in outputs)


def solution(mesh):
    in_specs = (
        P("freq", "tm", None, None, None),
        P("freq", None, None, None, None),
        P("freq", "tm", None),
        P("freq", "tm", None, None, None),
        P("freq", "tm", None, None, None),
    )
    out_specs = (
        P("freq", "tm", None, None, None),
        P("freq", "tm", None, None, None),
        P("freq", "tm", None, None, None),
    )
    return jax.shard_map(
        per_device, mesh=mesh, in_specs=in_specs, out_specs=out_specs, check_vma=False
    )
```

```python
import functools
import math

import jax
import jax.numpy as jnp
from jax import lax
from jax.experimental import pallas as pl
from jax.experimental.pallas import tpu as pltpu
from jax.sharding import PartitionSpec as P

LANES = 128
ROWS = 16
FREQ_ORDERS = 3
TIME_ORDERS = 2
MIB = 2**20

penalty = 1.0
f32 = jnp.float32


def poly_basis(length, position, order_count):
    centre = position - (length - 1) / 2.0
    linear = centre * (1.0 / math.sqrt(length * (length * length - 1) / 12.0))
    stacked = [jnp.ones_like(position) * (1.0 / math.sqrt(length)), linear]
    if order_count == 3:
        scale = math.sqrt(length * (length * length - 1) * (length * length - 4) / 180.0)
        stacked.append((centre * centre - (length * length - 1) / 12.0) * (1.0 / scale))
    return stacked


def whole_vmem(count):
    return [pl.BlockSpec(memory_space=pltpu.VMEM)] * count


def exchange(array, axis, distance):
    size = lax.axis_size(axis)
    return lax.ppermute(array, axis, [(place, place ^ distance) for place in range(size)])


def time_plan(distances):
    steps = []
    held, sums = 1, False
    for at in range(len(distances)):
        last = at == len(distances) - 1
        turn = not last and not sums and 2 * held > TIME_ORDERS and at < len(distances) - 2
        steps.append((held, sums, turn))
        if turn:
            held, sums = TIME_ORDERS, True
        elif not sums:
            held = 2 * held
    return steps


def time_weights(size, distances, index):
    weights = []

    def basis(place):
        return poly_basis(size, lax.convert_element_type(place, f32), TIME_ORDERS)

    def product(one, other):
        return sum(a * b for a, b in zip(basis(one), basis(other)))

    raw = [index]
    for at, (held, sums, turn) in enumerate(time_plan(distances)):
        if at == len(distances) - 1:
            for target in (index ^ distances[at], index):
                weights += basis(target) if sums else [product(target, place) for place in raw]
        elif not sums:
            raw = raw + [place ^ distances[at] for place in raw]
            if turn:
                for place in raw:
                    weights += basis(place)
    return weights


def time_weight_count(distances):
    total, raw = 0, 1
    for at, (held, sums, turn) in enumerate(time_plan(distances)):
        if at == len(distances) - 1:
            total += 2 * held
        elif not sums:
            raw = 2 * raw
            total += raw * TIME_ORDERS if turn else 0
    return total


def time_exchange(state, distances, weights, work):
    weights = list(weights)
    held = [state]
    for at, (_, sums, turn) in enumerate(time_plan(distances)):
        if at == len(distances) - 1:
            away, own = weights[: len(held)], weights[len(held) :]
            got = work(at, sum(w * a for w, a in zip(away, held)), distances[at])
            return held, own, got
        message = held[0] if len(held) == 1 else jnp.stack(held)
        got = work(at, message, distances[at])
        got = [got] if len(held) == 1 else [got[i] for i in range(len(held))]
        if sums:
            held = [a + b for a, b in zip(held, got)]
            continue
        held = held + got
        if turn:
            taken, weights = weights[: len(held) * TIME_ORDERS], weights[len(held) * TIME_ORDERS :]
            held = [sum(taken[i * TIME_ORDERS + j] * a for i, a in enumerate(held)) for j in range(TIME_ORDERS)]


def freq_gather(state):
    size = lax.axis_size("freq")
    if size <= 4:
        return [state] + [exchange(state, "freq", distance) for distance in range(1, size)]
    distance = 1
    while distance < size:
        state = jnp.concatenate([state, exchange(state, "freq", distance)], axis=0)
        distance *= 2
    return [state]


def turn(gains):
    flat = gains.reshape(-1, gains.shape[-1])
    padded = jnp.concatenate([flat, jnp.zeros((LANES - flat.shape[0], flat.shape[1]), f32)], axis=0)
    return padded.T


def sum_rows(out_ref, out_rows, rows, model_ref, vis_ref, masked_ref, turned_ref, square_ref=None, power_ref=None):
    directions, blocks = model_ref.shape[0], model_ref.shape[3] // LANES
    turned = turned_ref[rows, :]

    def along_lanes(column):
        return jnp.take_along_axis(turned, jnp.full((ROWS, LANES), column, jnp.int32), axis=1)

    def add(total, term):
        return term if total is None else total + term

    whole, by_imag, by_real = [None] * blocks, [None] * blocks, [None] * blocks
    moved = {}
    for k in range(directions):
        near_real, near_imag = along_lanes(k), along_lanes(directions + k)
        near_sum, near_gap = near_real + near_imag, near_imag - near_real
        for block in range(blocks):
            columns = pl.ds(block * LANES, LANES)
            model_real = model_ref[k, 0, rows, columns].astype(f32)
            model_imag = model_ref[k, 1, rows, columns].astype(f32)
            gain_real = masked_ref[0, k : k + 1, columns]
            gain_imag = masked_ref[1, k : k + 1, columns]
            real = model_real * gain_real + model_imag * gain_imag
            imag = model_imag * gain_real - model_real * gain_imag
            both = real + imag
            moved[k, block] = (real, imag, both)
            whole[block] = add(whole[block], near_real * both)
            by_imag[block] = add(by_imag[block], imag * near_sum)
            by_real[block] = add(by_real[block], real * near_gap)
    residuals = []
    for block in range(blocks):
        columns = pl.ds(block * LANES, LANES)
        real = vis_ref[0, rows, columns].astype(f32) - (whole[block] - by_imag[block])
        imag = vis_ref[1, rows, columns].astype(f32) - (whole[block] + by_real[block])
        residuals.append((real, imag + real, imag - real))
    for k in range(directions):
        shared = by_gap = by_sum = curvature = None
        for block in range(blocks):
            columns = pl.ds(block * LANES, LANES)
            real, imag, both = moved[k, block]
            resid_real, resid_sum, resid_gap = residuals[block]
            shared = add(shared, resid_real * both)
            by_gap = add(by_gap, imag * resid_gap)
            by_sum = add(by_sum, real * resid_sum)
            if square_ref is None:
                curvature = add(curvature, real * real + imag * imag)
            else:
                curvature = add(curvature, square_ref[k, rows, columns] * power_ref[k : k + 1, columns])
        for kind, total in enumerate((by_gap + shared, by_sum - shared, curvature)):
            place = kind * directions + k
            out_ref[out_rows, place : place + 1] = jnp.sum(total, axis=1, keepdims=True)


def part_kernel(start, unroll, *refs):
    *inputs, sums_ref = refs

    def step(at, carry):
        first = pl.multiple_of(at * ROWS, ROWS)
        rows = pl.ds(pl.multiple_of(start + first, ROWS), ROWS)
        sum_rows(sums_ref, pl.ds(first, ROWS), rows, *inputs)
        return carry

    lax.fori_loop(0, sums_ref.shape[0] // ROWS, step, 0, unroll=unroll)


def widen_kernel(model_ref, wide_ref, square_ref):
    def step(at, carry):
        rows = pl.ds(pl.multiple_of(at * ROWS, ROWS), ROWS)
        for k in range(model_ref.shape[0]):
            real, imag = model_ref[k, 0, rows, :].astype(f32), model_ref[k, 1, rows, :].astype(f32)
            wide_ref[k, 0, rows, :] = real
            wide_ref[k, 1, rows, :] = imag
            square_ref[k, rows, :] = real * real + imag * imag
        return carry

    lax.fori_loop(0, model_ref.shape[2] // ROWS, step, 0, unroll=2)


def setup_kernel(plan, gains_in, duals_in, flags_in, gains_ref, merged_ref, masked_ref, turned_ref, mask_ref, *refs):
    *weight_refs, duals_ref, flags_ref, sems = refs
    places = ((gains_in, gains_ref), (duals_in, duals_ref), (flags_in, flags_ref))
    copies = [pltpu.make_async_copy(source, target, sems.at[at]) for at, (source, target) in enumerate(places)]
    for copy in copies:
        copy.start()
    axis, size, distances = plan
    index = jnp.full((8, LANES), lax.axis_index(axis), jnp.int32)
    for ref, weight in zip(weight_refs, time_weights(size, distances, index)):
        ref[...] = jnp.broadcast_to(jnp.tile(weight, (ref.shape[1] // 8, ref.shape[2] // LANES))[None], ref.shape)
    for copy in copies:
        copy.wait()
    gains = gains_ref[...]
    mask = flags_ref[...].astype(f32)
    mask_ref[...] = mask
    merged_ref[...] = gains + duals_ref[...]
    masked_ref[...] = gains * mask[None]
    turned_ref[...] = turn(gains)


def transposed_sums(refs):
    return jnp.concatenate([ref[...] for ref in refs], axis=0).T


def projected(weight_refs, held_refs, got_ref):
    total = got_ref[...]
    for weight_ref, held_ref in zip(weight_refs, held_refs):
        total = total + weight_ref[...] * held_ref[...]
    return total


def middle_kernel(parts, terms, *refs):
    sums_refs, weight_refs, held_refs = refs[:parts], refs[parts : parts + terms], refs[parts + terms : parts + 2 * terms]
    got_ref, merged_ref, gains_ref, mask_ref, out_ref = refs[parts + 2 * terms :]
    sums = transposed_sums(sums_refs)
    mask = mask_ref[...]
    directions = gains_ref.shape[1]
    curvature = sums[2 * directions : 3 * directions] * mask
    inverse = 1.0 / (curvature + penalty)
    along_time = projected(weight_refs, held_refs, got_ref)
    for part in range(2):
        numer = sums[part * directions : (part + 1) * directions] * mask
        fixed = numer + curvature * gains_ref[part] - penalty * merged_ref[part]
        out_ref[0, part] = along_time[part]
        out_ref[0, 2 + part] = fixed * inverse
    out_ref[0, 4] = (2.0 * penalty) * inverse


def update_kernel(size, *refs):
    *gathered, merged_ref, mask_ref, gains_ref, duals_ref, along_ref, masked_ref, turned_ref, power_ref = refs
    rows, lanes = merged_ref.shape[1:]
    index = lax.axis_index("freq")
    held, bases = [], []
    for ref in gathered:
        for at in range(ref.shape[0]):
            held.append((ref, at))
            place = jnp.full((8, LANES), index ^ (len(held) - 1), jnp.int32).astype(f32)
            basis = poly_basis(size, place, FREQ_ORDERS)
            bases.append([jnp.tile(weight, (rows // 8, lanes // LANES)) for weight in basis])
    gains, duals, along = [], [], []
    for part in range(2):
        values = [ref[at, part] for ref, at in held]
        coeffs = [sum(basis[i] * value for basis, value in zip(bases, values)) for i in range(FREQ_ORDERS)]
        solved = []
        for (ref, at), basis in zip(held, bases):
            consensus = sum(weight * coeff for weight, coeff in zip(basis, coeffs))
            if not solved:
                duals.append(merged_ref[part] - consensus)
            solved.append(ref[at, 2 + part] + ref[at, 4] * consensus)
        coeffs = [sum(basis[i] * value for basis, value in zip(bases, solved)) for i in range(FREQ_ORDERS)]
        gains.append(solved[0])
        along.append(sum(weight * coeff for weight, coeff in zip(bases[0], coeffs)))
    gains = jnp.stack(gains)
    gains_ref[...] = gains
    duals_ref[...] = jnp.stack(duals)
    along_ref[...] = jnp.stack(along)
    masked = gains * mask_ref[...][None]
    masked_ref[...] = masked
    turned_ref[...] = turn(gains)
    power_ref[...] = masked[0] * masked[0] + masked[1] * masked[1]


def finish_kernel(parts, terms, *refs):
    sums_refs, weight_refs, held_refs = refs[:parts], refs[parts : parts + terms], refs[parts + terms : parts + 2 * terms]
    got_ref, gains_ref, duals_ref, mask_ref, solved_ref, consensus_ref, final_ref = refs[parts + 2 * terms :]
    sums = transposed_sums(sums_refs)
    gains = gains_ref[...]
    mask = mask_ref[...]
    directions = gains.shape[1]
    consensus = projected(weight_refs, held_refs, got_ref)
    duals = duals_ref[...] + gains - consensus
    target = consensus - duals
    curvature = sums[2 * directions : 3 * directions] * mask
    divisor = curvature + penalty
    for part in range(2):
        numer = sums[part * directions : (part + 1) * directions] * mask
        solved_ref[part] = (numer + curvature * gains[part] + penalty * target[part]) / divisor
    consensus_ref[...] = consensus
    final_ref[...] = duals


def cut(total, shares):
    ends, done = [0], 0.0
    for share in shares:
        done += share
        ends.append(round(total * done / sum(shares)))
    return [(a, b - a) for a, b in zip(ends, ends[1:])]


def per_device(visibilities, model_vis, station_flags, initial_gains, initial_duals):
    vis_block = visibilities[0, 0]
    model_block = model_vis[0]
    _, directions, receptors = initial_gains.shape[2:]
    state = jax.ShapeDtypeStruct((2, directions, receptors), f32)
    turned_shape = jax.ShapeDtypeStruct((receptors, LANES), f32)
    pairs = directions * receptors

    freq_count, time_count = lax.axis_size("freq"), lax.axis_size("tm")
    distances = [1 << b for b in reversed(range(time_count.bit_length() - 1))]
    steps = len(distances)
    units = receptors // ROWS

    def shares(first, middle, last):
        return ([first] + [middle] * (steps - 2) + [last])[-steps:]

    def sums_shape(length):
        return jax.ShapeDtypeStruct((length, LANES), f32)

    def cost(length):
        return pl.CostEstimate(flops=28 * pairs * length, bytes_accessed=4 * pairs * length, transcendentals=0)

    small = [initial_gains[0, 0], initial_duals[0, 0], station_flags[0]]
    gains, merged, masked, turned, mask, *weights = pl.pallas_call(
        functools.partial(setup_kernel, ("tm", time_count, distances)),
        out_shape=[state] * 3
        + [turned_shape, jax.ShapeDtypeStruct((1, receptors), f32)]
        + [state] * time_weight_count(distances),
        in_specs=[pl.BlockSpec(memory_space=pltpu.HBM)] * 3,
        out_specs=whole_vmem(5 + time_weight_count(distances)),
        scratch_shapes=[
            pltpu.VMEM(state.shape, f32),
            pltpu.VMEM((1, receptors), jnp.int32),
            pltpu.SemaphoreType.DMA((3,)),
        ],
        compiler_params=pltpu.CompilerParams(vmem_limit_bytes=4 * MIB),
        cost_estimate=pl.CostEstimate(flops=1 << 36, bytes_accessed=1 << 28, transcendentals=0),
        name="setup",
    )(*[pltpu.with_memory_space_constraint(one, pltpu.HBM) for one in small])

    def part(name, start, length, operands):
        return pl.pallas_call(
            functools.partial(part_kernel, start, True),
            out_shape=sums_shape(length),
            in_specs=whole_vmem(len(operands)),
            out_specs=pl.BlockSpec(memory_space=pltpu.VMEM),
            compiler_params=pltpu.CompilerParams(vmem_limit_bytes=3 * MIB),
            cost_estimate=cost(length),
            name=name,
        )(*operands)

    def worker(name, ranges, results, fixed, now):
        def work(at, message, distance):
            message, current = lax.optimization_barrier((message, now))
            got = exchange(message, "tm", distance)
            result = part(f"{name}{at}", *ranges[at], fixed[:2] + current[:2] + fixed[2:] + current[2:])
            got, result = lax.optimization_barrier((got, result))
            results.append(result)
            return got

        return work

    def small_kernel(kernel, name, operands, outs):
        return pl.pallas_call(
            kernel,
            out_shape=outs,
            in_specs=whole_vmem(len(operands)),
            out_specs=whole_vmem(len(outs)),
            compiler_params=pltpu.CompilerParams(vmem_limit_bytes=4 * MIB),
            name=name,
        )(*operands)

    beside = [(ROWS * a, ROWS * n) for a, n in cut(units, shares(15.0, 13.0, 4.0))]
    sums = []
    held, own, got = time_exchange(merged, distances, weights, worker("first", beside, sums, [model_block, vis_block], [masked, turned]))
    operands = sums + own + held + [got, merged, gains, mask]
    (payload,) = small_kernel(
        functools.partial(middle_kernel, len(sums), len(held)),
        "middle",
        operands,
        [jax.ShapeDtypeStruct((1, 5, directions, receptors), f32)],
    )
    payload, model_now = lax.optimization_barrier((payload, model_block))
    gathered = freq_gather(payload)
    model_wide, model_square = pl.pallas_call(
        widen_kernel,
        out_shape=[
            jax.ShapeDtypeStruct(model_block.shape, f32),
            jax.ShapeDtypeStruct((directions, receptors, receptors), f32),
        ],
        in_specs=whole_vmem(1),
        out_specs=whole_vmem(2),
        compiler_params=pltpu.CompilerParams(vmem_limit_bytes=3 * MIB),
        cost_estimate=pl.CostEstimate(flops=28 * pairs * 96, bytes_accessed=12 * pairs * receptors, transcendentals=0),
        name="widen",
    )(model_now)
    gathered, model_wide, model_square = lax.optimization_barrier((gathered, model_wide, model_square))
    gains, duals, along_freq, masked, turned, power = small_kernel(
        functools.partial(update_kernel, freq_count),
        "update",
        gathered + [merged, mask],
        [state] * 4 + [turned_shape, jax.ShapeDtypeStruct((directions, receptors), f32)],
    )

    beside = [(ROWS * a, ROWS * n) for a, n in cut(units, shares(12.0, 14.0, 6.0))]
    sums = []
    held, own, got = time_exchange(along_freq, distances, weights, worker("second", beside, sums, [model_wide, vis_block, model_square], [masked, turned, power]))
    operands = sums + own + held + [got, gains, duals, mask]
    outputs = small_kernel(functools.partial(finish_kernel, len(sums), len(held)), "finish", operands, [state] * 3)
    return tuple(out[None, None] for out in outputs)


def solution(mesh):
    in_specs = (
        P("freq", "tm", None, None, None),
        P("freq", None, None, None, None),
        P("freq", "tm", None),
        P("freq", "tm", None, None, None),
        P("freq", "tm", None, None, None),
    )
    out_specs = (
        P("freq", "tm", None, None, None),
        P("freq", "tm", None, None, None),
        P("freq", "tm", None, None, None),
    )
    return jax.shard_map(
        per_device, mesh=mesh, in_specs=in_specs, out_specs=out_specs, check_vma=False
    )
```

```python
import functools
import math

import jax
import jax.numpy as jnp
from jax import lax
from jax.experimental import pallas as pl
from jax.experimental.pallas import tpu as pltpu
from jax.sharding import PartitionSpec as P

LANES = 128
ROWS = 16
FREQ_ORDERS = 3
TIME_ORDERS = 2
MIB = 2**20

penalty = 1.0
f32 = jnp.float32


def poly_basis(length, position, order_count):
    centre = position - (length - 1) / 2.0
    linear = centre * (1.0 / math.sqrt(length * (length * length - 1) / 12.0))
    stacked = [jnp.ones_like(position) * (1.0 / math.sqrt(length)), linear]
    if order_count == 3:
        scale = math.sqrt(length * (length * length - 1) * (length * length - 4) / 180.0)
        stacked.append((centre * centre - (length * length - 1) / 12.0) * (1.0 / scale))
    return stacked


def whole_vmem(count):
    return [pl.BlockSpec(memory_space=pltpu.VMEM)] * count


def exchange(array, axis, distance):
    size = lax.axis_size(axis)
    return lax.ppermute(array, axis, [(place, place ^ distance) for place in range(size)])


def time_plan(distances):
    steps = []
    held, sums = 1, False
    for at in range(len(distances)):
        last = at == len(distances) - 1
        turn = not last and not sums and 2 * held > TIME_ORDERS and at < len(distances) - 2
        steps.append((held, sums, turn))
        if turn:
            held, sums = TIME_ORDERS, True
        elif not sums:
            held = 2 * held
    return steps


def time_weights(size, distances, index):
    weights = []

    def basis(place):
        return poly_basis(size, lax.convert_element_type(place, f32), TIME_ORDERS)

    def product(one, other):
        return sum(a * b for a, b in zip(basis(one), basis(other)))

    raw = [index]
    for at, (held, sums, turn) in enumerate(time_plan(distances)):
        if at == len(distances) - 1:
            for target in (index ^ distances[at], index):
                weights += basis(target) if sums else [product(target, place) for place in raw]
        elif not sums:
            raw = raw + [place ^ distances[at] for place in raw]
            if turn:
                for place in raw:
                    weights += basis(place)
    return weights


def time_weight_count(distances):
    total, raw = 0, 1
    for at, (held, sums, turn) in enumerate(time_plan(distances)):
        if at == len(distances) - 1:
            total += 2 * held
        elif not sums:
            raw = 2 * raw
            total += raw * TIME_ORDERS if turn else 0
    return total


def time_exchange(state, distances, weights, work):
    weights = list(weights)
    held = [state]
    for at, (_, sums, turn) in enumerate(time_plan(distances)):
        if at == len(distances) - 1:
            away, own = weights[: len(held)], weights[len(held) :]
            got = work(at, sum(w * a for w, a in zip(away, held)), distances[at])
            return held, own, got
        message = held[0] if len(held) == 1 else jnp.stack(held)
        got = work(at, message, distances[at])
        got = [got] if len(held) == 1 else [got[i] for i in range(len(held))]
        if sums:
            held = [a + b for a, b in zip(held, got)]
            continue
        held = held + got
        if turn:
            taken, weights = weights[: len(held) * TIME_ORDERS], weights[len(held) * TIME_ORDERS :]
            held = [sum(taken[i * TIME_ORDERS + j] * a for i, a in enumerate(held)) for j in range(TIME_ORDERS)]


def freq_gather(state):
    size = lax.axis_size("freq")
    if size <= 4:
        return [state] + [exchange(state, "freq", distance) for distance in range(1, size)]
    distance = 1
    while distance < size:
        state = jnp.concatenate([state, exchange(state, "freq", distance)], axis=0)
        distance *= 2
    return [state]


def turn(gains):
    flat = gains.reshape(-1, gains.shape[-1])
    padded = jnp.concatenate([flat, jnp.zeros((LANES - flat.shape[0], flat.shape[1]), f32)], axis=0)
    return padded.T


def sum_rows(rows, model_ref, vis_ref, masked_ref, turned_ref, square_ref=None, power_ref=None):
    directions, blocks = model_ref.shape[0], model_ref.shape[3] // LANES
    turned = turned_ref[rows, :]

    def along_lanes(column):
        return jnp.take_along_axis(turned, jnp.full((ROWS, LANES), column, jnp.int32), axis=1)

    def add(total, term):
        return term if total is None else total + term

    whole, by_imag, by_real = [None] * blocks, [None] * blocks, [None] * blocks
    moved = {}
    for k in range(directions):
        near_real, near_imag = along_lanes(k), along_lanes(directions + k)
        near_sum, near_gap = near_real + near_imag, near_imag - near_real
        for block in range(blocks):
            columns = pl.ds(block * LANES, LANES)
            model_real = model_ref[k, 0, rows, columns].astype(f32)
            model_imag = model_ref[k, 1, rows, columns].astype(f32)
            gain_real = masked_ref[0, k : k + 1, columns]
            gain_imag = masked_ref[1, k : k + 1, columns]
            real = model_real * gain_real + model_imag * gain_imag
            imag = model_imag * gain_real - model_real * gain_imag
            both = real + imag
            moved[k, block] = (real, imag, both)
            whole[block] = add(whole[block], near_real * both)
            by_imag[block] = add(by_imag[block], imag * near_sum)
            by_real[block] = add(by_real[block], real * near_gap)
    residuals = []
    for block in range(blocks):
        columns = pl.ds(block * LANES, LANES)
        real = vis_ref[0, rows, columns].astype(f32) - (whole[block] - by_imag[block])
        imag = vis_ref[1, rows, columns].astype(f32) - (whole[block] + by_real[block])
        residuals.append((real, imag + real, imag - real))
    found = []
    for k in range(directions):
        shared = by_gap = by_sum = curvature = None
        for block in range(blocks):
            columns = pl.ds(block * LANES, LANES)
            real, imag, both = moved[k, block]
            resid_real, resid_sum, resid_gap = residuals[block]
            shared = add(shared, resid_real * both)
            by_gap = add(by_gap, imag * resid_gap)
            by_sum = add(by_sum, real * resid_sum)
            if square_ref is None:
                curvature = add(curvature, real * real + imag * imag)
            else:
                curvature = add(curvature, square_ref[k, rows, columns] * power_ref[k : k + 1, columns])
        for kind, total in enumerate((by_gap + shared, by_sum - shared, curvature)):
            found.append((kind * directions + k, jnp.sum(total, axis=1, keepdims=True)))
    return found


def part_kernel(start, late, *refs):
    *inputs, sums_ref = refs
    lane = lax.broadcasted_iota(jnp.int32, (ROWS, LANES), 1)
    waiting = None
    for first in range(0, sums_ref.shape[0], ROWS):
        here = pl.ds(first, ROWS)
        found = sum_rows(pl.ds(start + first, ROWS), *inputs)
        if not late:
            for place, total in found:
                sums_ref[here, place : place + 1] = total
            continue
        row = jnp.zeros((ROWS, LANES), f32)
        for place, total in found:
            row = jnp.where(lane == place, total, row)
        if waiting is not None:
            sums_ref[waiting[0], :] = waiting[1]
        waiting = here, row
    if waiting is not None:
        sums_ref[waiting[0], :] = waiting[1]


def widen_kernel(model_ref, wide_ref, square_ref):
    def step(at, carry):
        rows = pl.ds(pl.multiple_of(at * ROWS, ROWS), ROWS)
        for k in range(model_ref.shape[0]):
            real, imag = model_ref[k, 0, rows, :].astype(f32), model_ref[k, 1, rows, :].astype(f32)
            wide_ref[k, 0, rows, :] = real
            wide_ref[k, 1, rows, :] = imag
            square_ref[k, rows, :] = real * real + imag * imag
        return carry

    lax.fori_loop(0, model_ref.shape[2] // ROWS, step, 0, unroll=2)


def setup_kernel(plan, gains_in, duals_in, flags_in, gains_ref, merged_ref, masked_ref, turned_ref, mask_ref, *refs):
    *weight_refs, duals_ref, flags_ref, sems = refs
    places = ((gains_in, gains_ref), (duals_in, duals_ref), (flags_in, flags_ref))
    copies = [pltpu.make_async_copy(source, target, sems.at[at]) for at, (source, target) in enumerate(places)]
    for copy in copies:
        copy.start()
    axis, size, distances = plan
    index = jnp.full((8, LANES), lax.axis_index(axis), jnp.int32)
    for ref, weight in zip(weight_refs, time_weights(size, distances, index)):
        ref[...] = jnp.broadcast_to(jnp.tile(weight, (ref.shape[1] // 8, ref.shape[2] // LANES))[None], ref.shape)
    for copy in copies:
        copy.wait()
    gains = gains_ref[...]
    mask = flags_ref[...].astype(f32)
    mask_ref[...] = mask
    merged_ref[...] = gains + duals_ref[...]
    masked_ref[...] = gains * mask[None]
    turned_ref[...] = turn(gains)


def transposed_sums(refs):
    return jnp.concatenate([ref[...] for ref in refs], axis=0).T


def projected(weight_refs, held_refs, got_ref):
    total = got_ref[...]
    for weight_ref, held_ref in zip(weight_refs, held_refs):
        total = total + weight_ref[...] * held_ref[...]
    return total


def middle_kernel(parts, terms, *refs):
    sums_refs, weight_refs, held_refs = refs[:parts], refs[parts : parts + terms], refs[parts + terms : parts + 2 * terms]
    got_ref, merged_ref, gains_ref, mask_ref, out_ref = refs[parts + 2 * terms :]
    sums = transposed_sums(sums_refs)
    mask = mask_ref[...]
    directions = gains_ref.shape[1]
    curvature = sums[2 * directions : 3 * directions] * mask
    inverse = 1.0 / (curvature + penalty)
    along_time = projected(weight_refs, held_refs, got_ref)
    for part in range(2):
        numer = sums[part * directions : (part + 1) * directions] * mask
        fixed = numer + curvature * gains_ref[part] - penalty * merged_ref[part]
        out_ref[0, part] = along_time[part]
        out_ref[0, 2 + part] = fixed * inverse
    out_ref[0, 4] = (2.0 * penalty) * inverse


def update_kernel(size, *refs):
    *gathered, merged_ref, mask_ref, gains_ref, duals_ref, along_ref, masked_ref, turned_ref, power_ref = refs
    rows, lanes = merged_ref.shape[1:]
    index = lax.axis_index("freq")
    held, bases = [], []
    for ref in gathered:
        for at in range(ref.shape[0]):
            held.append((ref, at))
            place = jnp.full((8, LANES), index ^ (len(held) - 1), jnp.int32).astype(f32)
            basis = poly_basis(size, place, FREQ_ORDERS)
            bases.append([jnp.tile(weight, (rows // 8, lanes // LANES)) for weight in basis])
    gains, duals, along = [], [], []
    for part in range(2):
        values = [ref[at, part] for ref, at in held]
        coeffs = [sum(basis[i] * value for basis, value in zip(bases, values)) for i in range(FREQ_ORDERS)]
        solved = []
        for (ref, at), basis in zip(held, bases):
            consensus = sum(weight * coeff for weight, coeff in zip(basis, coeffs))
            if not solved:
                duals.append(merged_ref[part] - consensus)
            solved.append(ref[at, 2 + part] + ref[at, 4] * consensus)
        coeffs = [sum(basis[i] * value for basis, value in zip(bases, solved)) for i in range(FREQ_ORDERS)]
        gains.append(solved[0])
        along.append(sum(weight * coeff for weight, coeff in zip(bases[0], coeffs)))
    gains = jnp.stack(gains)
    gains_ref[...] = gains
    duals_ref[...] = jnp.stack(duals)
    along_ref[...] = jnp.stack(along)
    masked = gains * mask_ref[...][None]
    masked_ref[...] = masked
    turned_ref[...] = turn(gains)
    power_ref[...] = masked[0] * masked[0] + masked[1] * masked[1]


def finish_kernel(parts, terms, *refs):
    sums_refs, weight_refs, held_refs = refs[:parts], refs[parts : parts + terms], refs[parts + terms : parts + 2 * terms]
    got_ref, gains_ref, duals_ref, mask_ref, solved_ref, consensus_ref, final_ref = refs[parts + 2 * terms :]
    sums = transposed_sums(sums_refs)
    gains = gains_ref[...]
    mask = mask_ref[...]
    directions = gains.shape[1]
    consensus = projected(weight_refs, held_refs, got_ref)
    duals = duals_ref[...] + gains - consensus
    target = consensus - duals
    curvature = sums[2 * directions : 3 * directions] * mask
    divisor = curvature + penalty
    for part in range(2):
        numer = sums[part * directions : (part + 1) * directions] * mask
        solved_ref[part] = (numer + curvature * gains[part] + penalty * target[part]) / divisor
    consensus_ref[...] = consensus
    final_ref[...] = duals


def cut(total, shares):
    ends, done = [0], 0.0
    for share in shares:
        done += share
        ends.append(round(total * done / sum(shares)))
    return [(a, b - a) for a, b in zip(ends, ends[1:])]


def per_device(visibilities, model_vis, station_flags, initial_gains, initial_duals):
    vis_block = visibilities[0, 0]
    model_block = model_vis[0]
    _, directions, receptors = initial_gains.shape[2:]
    state = jax.ShapeDtypeStruct((2, directions, receptors), f32)
    turned_shape = jax.ShapeDtypeStruct((receptors, LANES), f32)
    pairs = directions * receptors

    freq_count, time_count = lax.axis_size("freq"), lax.axis_size("tm")
    distances = [1 << b for b in reversed(range(time_count.bit_length() - 1))]
    steps = len(distances)
    units = receptors // ROWS

    def shares(first, middle, last):
        return ([first] + [middle] * (steps - 2) + [last])[-steps:]

    def sums_shape(length):
        return jax.ShapeDtypeStruct((length, LANES), f32)

    def cost(length):
        return pl.CostEstimate(flops=28 * pairs * length, bytes_accessed=4 * pairs * length, transcendentals=0)

    small = [initial_gains[0, 0], initial_duals[0, 0], station_flags[0]]
    gains, merged, masked, turned, mask, *weights = pl.pallas_call(
        functools.partial(setup_kernel, ("tm", time_count, distances)),
        out_shape=[state] * 3
        + [turned_shape, jax.ShapeDtypeStruct((1, receptors), f32)]
        + [state] * time_weight_count(distances),
        in_specs=[pl.BlockSpec(memory_space=pltpu.HBM)] * 3,
        out_specs=whole_vmem(5 + time_weight_count(distances)),
        scratch_shapes=[
            pltpu.VMEM(state.shape, f32),
            pltpu.VMEM((1, receptors), jnp.int32),
            pltpu.SemaphoreType.DMA((3,)),
        ],
        compiler_params=pltpu.CompilerParams(vmem_limit_bytes=4 * MIB),
        cost_estimate=pl.CostEstimate(flops=1 << 36, bytes_accessed=1 << 28, transcendentals=0),
        name="setup",
    )(*[pltpu.with_memory_space_constraint(one, pltpu.HBM) for one in small])

    def part(name, start, length, operands):
        return pl.pallas_call(
            functools.partial(part_kernel, start, len(operands) > 4),
            out_shape=sums_shape(length),
            in_specs=whole_vmem(len(operands)),
            out_specs=pl.BlockSpec(memory_space=pltpu.VMEM),
            compiler_params=pltpu.CompilerParams(vmem_limit_bytes=3 * MIB),
            cost_estimate=cost(length),
            name=name,
        )(*operands)

    def worker(name, ranges, results, fixed, now):
        def work(at, message, distance):
            message, current = lax.optimization_barrier((message, now))
            got = exchange(message, "tm", distance)
            result = part(f"{name}{at}", *ranges[at], fixed[:2] + current[:2] + fixed[2:] + current[2:])
            got, result = lax.optimization_barrier((got, result))
            results.append(result)
            return got

        return work

    def small_kernel(kernel, name, operands, outs):
        return pl.pallas_call(
            kernel,
            out_shape=outs,
            in_specs=whole_vmem(len(operands)),
            out_specs=whole_vmem(len(outs)),
            compiler_params=pltpu.CompilerParams(vmem_limit_bytes=4 * MIB),
            name=name,
        )(*operands)

    beside = [(ROWS * a, ROWS * n) for a, n in cut(units, shares(15.0, 13.0, 4.0))]
    sums = []
    held, own, got = time_exchange(merged, distances, weights, worker("first", beside, sums, [model_block, vis_block], [masked, turned]))
    operands = sums + own + held + [got, merged, gains, mask]
    (payload,) = small_kernel(
        functools.partial(middle_kernel, len(sums), len(held)),
        "middle",
        operands,
        [jax.ShapeDtypeStruct((1, 5, directions, receptors), f32)],
    )
    payload, model_now = lax.optimization_barrier((payload, model_block))
    gathered = freq_gather(payload)
    model_wide, model_square = pl.pallas_call(
        widen_kernel,
        out_shape=[
            jax.ShapeDtypeStruct(model_block.shape, f32),
            jax.ShapeDtypeStruct((directions, receptors, receptors), f32),
        ],
        in_specs=whole_vmem(1),
        out_specs=whole_vmem(2),
        compiler_params=pltpu.CompilerParams(vmem_limit_bytes=3 * MIB),
        cost_estimate=pl.CostEstimate(flops=28 * pairs * 96, bytes_accessed=12 * pairs * receptors, transcendentals=0),
        name="widen",
    )(model_now)
    gathered, model_wide, model_square = lax.optimization_barrier((gathered, model_wide, model_square))
    gains, duals, along_freq, masked, turned, power = small_kernel(
        functools.partial(update_kernel, freq_count),
        "update",
        gathered + [merged, mask],
        [state] * 4 + [turned_shape, jax.ShapeDtypeStruct((directions, receptors), f32)],
    )

    beside = [(ROWS * a, ROWS * n) for a, n in cut(units, shares(12.0, 14.0, 6.0))]
    sums = []
    held, own, got = time_exchange(along_freq, distances, weights, worker("second", beside, sums, [model_wide, vis_block, model_square], [masked, turned, power]))
    operands = sums + own + held + [got, gains, duals, mask]
    outputs = small_kernel(functools.partial(finish_kernel, len(sums), len(held)), "finish", operands, [state] * 3)
    return tuple(out[None, None] for out in outputs)


def solution(mesh):
    in_specs = (
        P("freq", "tm", None, None, None),
        P("freq", None, None, None, None),
        P("freq", "tm", None),
        P("freq", "tm", None, None, None),
        P("freq", "tm", None, None, None),
    )
    out_specs = (
        P("freq", "tm", None, None, None),
        P("freq", "tm", None, None, None),
        P("freq", "tm", None, None, None),
    )
    return jax.shard_map(
        per_device, mesh=mesh, in_specs=in_specs, out_specs=out_specs, check_vma=False
    )
```

```python
import functools
import math

import jax
import jax.numpy as jnp
from jax import lax
from jax.experimental import pallas as pl
from jax.experimental.pallas import tpu as pltpu
from jax.sharding import PartitionSpec as P

LANES = 128
ROWS = 16
FREQ_ORDERS = 3
TIME_ORDERS = 2
MIB = 2**20

penalty = 1.0
f32 = jnp.float32


def poly_basis(length, position, order_count):
    centre = position - (length - 1) / 2.0
    linear = centre * (1.0 / math.sqrt(length * (length * length - 1) / 12.0))
    stacked = [jnp.ones_like(position) * (1.0 / math.sqrt(length)), linear]
    if order_count == 3:
        scale = math.sqrt(length * (length * length - 1) * (length * length - 4) / 180.0)
        stacked.append((centre * centre - (length * length - 1) / 12.0) * (1.0 / scale))
    return stacked


def whole_vmem(count):
    return [pl.BlockSpec(memory_space=pltpu.VMEM)] * count


def exchange(array, axis, distance):
    size = lax.axis_size(axis)
    return lax.ppermute(array, axis, [(place, place ^ distance) for place in range(size)])


def time_plan(distances):
    steps = []
    held, sums = 1, False
    for at in range(len(distances)):
        last = at == len(distances) - 1
        turn = not last and not sums and 2 * held > TIME_ORDERS and at < len(distances) - 2
        steps.append((held, sums, turn))
        if turn:
            held, sums = TIME_ORDERS, True
        elif not sums:
            held = 2 * held
    return steps


def time_weights(size, distances, index):
    weights = []

    def basis(place):
        return poly_basis(size, lax.convert_element_type(place, f32), TIME_ORDERS)

    def product(one, other):
        return sum(a * b for a, b in zip(basis(one), basis(other)))

    raw = [index]
    for at, (held, sums, turn) in enumerate(time_plan(distances)):
        if at == len(distances) - 1:
            for target in (index ^ distances[at], index):
                weights += basis(target) if sums else [product(target, place) for place in raw]
        elif not sums:
            raw = raw + [place ^ distances[at] for place in raw]
            if turn:
                for place in raw:
                    weights += basis(place)
    return weights


def time_weight_count(distances):
    total, raw = 0, 1
    for at, (held, sums, turn) in enumerate(time_plan(distances)):
        if at == len(distances) - 1:
            total += 2 * held
        elif not sums:
            raw = 2 * raw
            total += raw * TIME_ORDERS if turn else 0
    return total


def time_exchange(state, distances, weights, work):
    weights = list(weights)
    held = [state]
    for at, (_, sums, turn) in enumerate(time_plan(distances)):
        if at == len(distances) - 1:
            away, own = weights[: len(held)], weights[len(held) :]
            got = work(at, sum(w * a for w, a in zip(away, held)), distances[at])
            return held, own, got
        message = held[0] if len(held) == 1 else jnp.stack(held)
        got = work(at, message, distances[at])
        got = [got] if len(held) == 1 else [got[i] for i in range(len(held))]
        if sums:
            held = [a + b for a, b in zip(held, got)]
            continue
        held = held + got
        if turn:
            taken, weights = weights[: len(held) * TIME_ORDERS], weights[len(held) * TIME_ORDERS :]
            held = [sum(taken[i * TIME_ORDERS + j] * a for i, a in enumerate(held)) for j in range(TIME_ORDERS)]


def freq_gather(state):
    size = lax.axis_size("freq")
    if size <= 4:
        return [state] + [exchange(state, "freq", distance) for distance in range(1, size)]
    distance = 1
    while distance < size:
        state = jnp.concatenate([state, exchange(state, "freq", distance)], axis=0)
        distance *= 2
    return [state]


def turn(gains):
    flat = gains.reshape(-1, gains.shape[-1])
    padded = jnp.concatenate([flat, jnp.zeros((LANES - flat.shape[0], flat.shape[1]), f32)], axis=0)
    return padded.T


def sum_rows(rows, model_ref, vis_ref, masked_ref, turned_ref, square_ref=None, power_ref=None):
    directions, blocks = model_ref.shape[0], model_ref.shape[3] // LANES
    turned = turned_ref[rows, :]

    def along_lanes(column):
        return jnp.take_along_axis(turned, jnp.full((ROWS, LANES), column, jnp.int32), axis=1)

    def add(total, term):
        return term if total is None else total + term

    whole, by_imag, by_real = [None] * blocks, [None] * blocks, [None] * blocks
    moved = {}
    for k in range(directions):
        near_real, near_imag = along_lanes(k), along_lanes(directions + k)
        near_sum, near_gap = near_real + near_imag, near_imag - near_real
        for block in range(blocks):
            columns = pl.ds(block * LANES, LANES)
            model_real = model_ref[k, 0, rows, columns].astype(f32)
            model_imag = model_ref[k, 1, rows, columns].astype(f32)
            gain_real = masked_ref[0, k : k + 1, columns]
            gain_imag = masked_ref[1, k : k + 1, columns]
            real = model_real * gain_real + model_imag * gain_imag
            imag = model_imag * gain_real - model_real * gain_imag
            both = real + imag
            moved[k, block] = (real, imag, both)
            whole[block] = add(whole[block], near_real * both)
            by_imag[block] = add(by_imag[block], imag * near_sum)
            by_real[block] = add(by_real[block], real * near_gap)
    residuals = []
    for block in range(blocks):
        columns = pl.ds(block * LANES, LANES)
        real = vis_ref[0, rows, columns].astype(f32) - (whole[block] - by_imag[block])
        imag = vis_ref[1, rows, columns].astype(f32) - (whole[block] + by_real[block])
        residuals.append((real, imag + real, imag - real))
    found = []
    for k in range(directions):
        shared = by_gap = by_sum = curvature = None
        for block in range(blocks):
            columns = pl.ds(block * LANES, LANES)
            real, imag, both = moved[k, block]
            resid_real, resid_sum, resid_gap = residuals[block]
            shared = add(shared, resid_real * both)
            by_gap = add(by_gap, imag * resid_gap)
            by_sum = add(by_sum, real * resid_sum)
            if square_ref is None:
                curvature = add(curvature, real * real + imag * imag)
            else:
                curvature = add(curvature, square_ref[k, rows, columns] * power_ref[k : k + 1, columns])
        for kind, total in enumerate((by_gap + shared, by_sum - shared, curvature)):
            found.append((kind * directions + k, jnp.sum(total, axis=1, keepdims=True)))
    return found


def part_kernel(start, late, *refs):
    *inputs, sums_ref = refs
    lane = lax.broadcasted_iota(jnp.int32, (ROWS, LANES), 1)
    waiting = None
    for first in range(0, sums_ref.shape[0], ROWS):
        here = pl.ds(first, ROWS)
        found = sum_rows(pl.ds(start + first, ROWS), *inputs)
        if not late:
            for place, total in found:
                sums_ref[here, place : place + 1] = total
            continue
        row = jnp.zeros((ROWS, LANES), f32)
        for place, total in found:
            row = jnp.where(lane == place, total, row)
        if waiting is not None:
            sums_ref[waiting[0], :] = waiting[1]
        waiting = here, row
    if waiting is not None:
        sums_ref[waiting[0], :] = waiting[1]


def widen_kernel(model_ref, wide_ref, square_ref):
    def step(at, carry):
        rows = pl.ds(pl.multiple_of(at * ROWS, ROWS), ROWS)
        for k in range(model_ref.shape[0]):
            real, imag = model_ref[k, 0, rows, :].astype(f32), model_ref[k, 1, rows, :].astype(f32)
            wide_ref[k, 0, rows, :] = real
            wide_ref[k, 1, rows, :] = imag
            square_ref[k, rows, :] = real * real + imag * imag
        return carry

    lax.fori_loop(0, model_ref.shape[2] // ROWS, step, 0, unroll=2)


def setup_kernel(plan, gains_in, duals_in, flags_in, gains_ref, merged_ref, masked_ref, turned_ref, mask_ref, *refs):
    *weight_refs, duals_ref, flags_ref, sems = refs
    places = ((gains_in, gains_ref), (duals_in, duals_ref), (flags_in, flags_ref))
    copies = [pltpu.make_async_copy(source, target, sems.at[at]) for at, (source, target) in enumerate(places)]
    for copy in copies:
        copy.start()
    axis, size, distances = plan
    index = jnp.full((8, LANES), lax.axis_index(axis), jnp.int32)
    for ref, weight in zip(weight_refs, time_weights(size, distances, index)):
        ref[...] = jnp.broadcast_to(jnp.tile(weight, (ref.shape[1] // 8, ref.shape[2] // LANES))[None], ref.shape)
    for copy in copies:
        copy.wait()
    gains = gains_ref[...]
    mask = flags_ref[...].astype(f32)
    mask_ref[...] = mask
    merged_ref[...] = gains + duals_ref[...]
    masked_ref[...] = gains * mask[None]
    turned_ref[...] = turn(gains)


def transposed_sums(refs):
    return jnp.concatenate([ref[...] for ref in refs], axis=0).T


def projected(weight_refs, held_refs, got_ref):
    total = got_ref[...]
    for weight_ref, held_ref in zip(weight_refs, held_refs):
        total = total + weight_ref[...] * held_ref[...]
    return total


def middle_kernel(parts, terms, *refs):
    sums_refs, weight_refs, held_refs = refs[:parts], refs[parts : parts + terms], refs[parts + terms : parts + 2 * terms]
    got_ref, merged_ref, gains_ref, mask_ref, out_ref = refs[parts + 2 * terms :]
    sums = transposed_sums(sums_refs)
    mask = mask_ref[...]
    directions = gains_ref.shape[1]
    curvature = sums[2 * directions : 3 * directions] * mask
    inverse = 1.0 / (curvature + penalty)
    along_time = projected(weight_refs, held_refs, got_ref)
    for part in range(2):
        numer = sums[part * directions : (part + 1) * directions] * mask
        fixed = numer + curvature * gains_ref[part] - penalty * merged_ref[part]
        out_ref[0, part] = along_time[part]
        out_ref[0, 2 + part] = fixed * inverse
    out_ref[0, 4] = (2.0 * penalty) * inverse


def update_kernel(size, *refs):
    *gathered, merged_ref, mask_ref, gains_ref, duals_ref, along_ref, masked_ref, turned_ref, power_ref = refs
    rows, lanes = merged_ref.shape[1:]
    index = lax.axis_index("freq")
    held, bases = [], []
    for ref in gathered:
        for at in range(ref.shape[0]):
            held.append((ref, at))
            place = jnp.full((8, LANES), index ^ (len(held) - 1), jnp.int32).astype(f32)
            basis = poly_basis(size, place, FREQ_ORDERS)
            bases.append([jnp.tile(weight, (rows // 8, lanes // LANES)) for weight in basis])
    gains, duals, along = [], [], []
    for part in range(2):
        values = [ref[at, part] for ref, at in held]
        coeffs = [sum(basis[i] * value for basis, value in zip(bases, values)) for i in range(FREQ_ORDERS)]
        solved = []
        for (ref, at), basis in zip(held, bases):
            consensus = sum(weight * coeff for weight, coeff in zip(basis, coeffs))
            if not solved:
                duals.append(merged_ref[part] - consensus)
            solved.append(ref[at, 2 + part] + ref[at, 4] * consensus)
        coeffs = [sum(basis[i] * value for basis, value in zip(bases, solved)) for i in range(FREQ_ORDERS)]
        gains.append(solved[0])
        along.append(sum(weight * coeff for weight, coeff in zip(bases[0], coeffs)))
    gains = jnp.stack(gains)
    gains_ref[...] = gains
    duals_ref[...] = jnp.stack(duals)
    along_ref[...] = jnp.stack(along)
    masked = gains * mask_ref[...][None]
    masked_ref[...] = masked
    turned_ref[...] = turn(gains)
    power_ref[...] = masked[0] * masked[0] + masked[1] * masked[1]


def finish_kernel(parts, terms, *refs):
    sums_refs, weight_refs, held_refs = refs[:parts], refs[parts : parts + terms], refs[parts + terms : parts + 2 * terms]
    got_ref, gains_ref, duals_ref, mask_ref, solved_ref, consensus_ref, final_ref = refs[parts + 2 * terms :]
    sums = transposed_sums(sums_refs)
    gains = gains_ref[...]
    mask = mask_ref[...]
    directions = gains.shape[1]
    consensus = projected(weight_refs, held_refs, got_ref)
    duals = duals_ref[...] + gains - consensus
    target = consensus - duals
    curvature = sums[2 * directions : 3 * directions] * mask
    divisor = curvature + penalty
    for part in range(2):
        numer = sums[part * directions : (part + 1) * directions] * mask
        solved_ref[part] = (numer + curvature * gains[part] + penalty * target[part]) / divisor
    consensus_ref[...] = consensus
    final_ref[...] = duals


def cut(total, shares):
    ends, done = [0], 0.0
    for share in shares:
        done += share
        ends.append(round(total * done / sum(shares)))
    return [(a, b - a) for a, b in zip(ends, ends[1:])]


def per_device(visibilities, model_vis, station_flags, initial_gains, initial_duals):
    vis_block = visibilities[0, 0]
    model_block = model_vis[0]
    _, directions, receptors = initial_gains.shape[2:]
    state = jax.ShapeDtypeStruct((2, directions, receptors), f32)
    turned_shape = jax.ShapeDtypeStruct((receptors, LANES), f32)
    pairs = directions * receptors

    freq_count, time_count = lax.axis_size("freq"), lax.axis_size("tm")
    distances = [1 << b for b in reversed(range(time_count.bit_length() - 1))]
    distances[-2:] = distances[-2:][::-1]
    steps = len(distances)
    units = receptors // ROWS

    def shares(first, middle, last):
        return ([first] + [middle] * (steps - 2) + [last])[-steps:]

    def sums_shape(length):
        return jax.ShapeDtypeStruct((length, LANES), f32)

    def cost(length):
        return pl.CostEstimate(flops=28 * pairs * length, bytes_accessed=4 * pairs * length, transcendentals=0)

    small = [initial_gains[0, 0], initial_duals[0, 0], station_flags[0]]
    gains, merged, masked, turned, mask, *weights = pl.pallas_call(
        functools.partial(setup_kernel, ("tm", time_count, distances)),
        out_shape=[state] * 3
        + [turned_shape, jax.ShapeDtypeStruct((1, receptors), f32)]
        + [state] * time_weight_count(distances),
        in_specs=[pl.BlockSpec(memory_space=pltpu.HBM)] * 3,
        out_specs=whole_vmem(5 + time_weight_count(distances)),
        scratch_shapes=[
            pltpu.VMEM(state.shape, f32),
            pltpu.VMEM((1, receptors), jnp.int32),
            pltpu.SemaphoreType.DMA((3,)),
        ],
        compiler_params=pltpu.CompilerParams(vmem_limit_bytes=4 * MIB),
        cost_estimate=pl.CostEstimate(flops=1 << 36, bytes_accessed=1 << 28, transcendentals=0),
        name="setup",
    )(*[pltpu.with_memory_space_constraint(one, pltpu.HBM) for one in small])

    def part(name, start, length, operands):
        return pl.pallas_call(
            functools.partial(part_kernel, start, len(operands) > 4),
            out_shape=sums_shape(length),
            in_specs=whole_vmem(len(operands)),
            out_specs=pl.BlockSpec(memory_space=pltpu.VMEM),
            compiler_params=pltpu.CompilerParams(vmem_limit_bytes=3 * MIB),
            cost_estimate=cost(length),
            name=name,
        )(*operands)

    def worker(name, ranges, results, fixed, now):
        def work(at, message, distance):
            message, current = lax.optimization_barrier((message, now))
            got = exchange(message, "tm", distance)
            result = part(f"{name}{at}", *ranges[at], fixed[:2] + current[:2] + fixed[2:] + current[2:])
            got, result = lax.optimization_barrier((got, result))
            results.append(result)
            return got

        return work

    def small_kernel(kernel, name, operands, outs):
        return pl.pallas_call(
            kernel,
            out_shape=outs,
            in_specs=whole_vmem(len(operands)),
            out_specs=whole_vmem(len(outs)),
            compiler_params=pltpu.CompilerParams(vmem_limit_bytes=4 * MIB),
            name=name,
        )(*operands)

    beside = [(ROWS * a, ROWS * n) for a, n in cut(units, shares(12.0, 5.0, 15.0))]
    sums = []
    held, own, got = time_exchange(merged, distances, weights, worker("first", beside, sums, [model_block, vis_block], [masked, turned]))
    operands = sums + own + held + [got, merged, gains, mask]
    (payload,) = small_kernel(
        functools.partial(middle_kernel, len(sums), len(held)),
        "middle",
        operands,
        [jax.ShapeDtypeStruct((1, 5, directions, receptors), f32)],
    )
    payload, model_now = lax.optimization_barrier((payload, model_block))
    gathered = freq_gather(payload)
    model_wide, model_square = pl.pallas_call(
        widen_kernel,
        out_shape=[
            jax.ShapeDtypeStruct(model_block.shape, f32),
            jax.ShapeDtypeStruct((directions, receptors, receptors), f32),
        ],
        in_specs=whole_vmem(1),
        out_specs=whole_vmem(2),
        compiler_params=pltpu.CompilerParams(vmem_limit_bytes=3 * MIB),
        cost_estimate=pl.CostEstimate(flops=28 * pairs * 96, bytes_accessed=12 * pairs * receptors, transcendentals=0),
        name="widen",
    )(model_now)
    gathered, model_wide, model_square = lax.optimization_barrier((gathered, model_wide, model_square))
    gains, duals, along_freq, masked, turned, power = small_kernel(
        functools.partial(update_kernel, freq_count),
        "update",
        gathered + [merged, mask],
        [state] * 4 + [turned_shape, jax.ShapeDtypeStruct((directions, receptors), f32)],
    )

    beside = [(ROWS * a, ROWS * n) for a, n in cut(units, shares(11.0, 6.0, 15.0))]
    sums = []
    held, own, got = time_exchange(along_freq, distances, weights, worker("second", beside, sums, [model_wide, vis_block, model_square], [masked, turned, power]))
    operands = sums + own + held + [got, gains, duals, mask]
    outputs = small_kernel(functools.partial(finish_kernel, len(sums), len(held)), "finish", operands, [state] * 3)
    return tuple(out[None, None] for out in outputs)


def solution(mesh):
    in_specs = (
        P("freq", "tm", None, None, None),
        P("freq", None, None, None, None),
        P("freq", "tm", None),
        P("freq", "tm", None, None, None),
        P("freq", "tm", None, None, None),
    )
    out_specs = (
        P("freq", "tm", None, None, None),
        P("freq", "tm", None, None, None),
        P("freq", "tm", None, None, None),
    )
    return jax.shard_map(
        per_device, mesh=mesh, in_specs=in_specs, out_specs=out_specs, check_vma=False
    )
```
